256 devices in a mesh: node: 32 (over z, y), feat: 8 (over x, core).
Axes of the slice: x: 4, y: 4, z: 8, core: 2. Of those that a mesh axis runs over, the one named last changes fastest.
Arguments:
- batch_node_input: bfloat16 [49152, 1024], P('node', 'feat'), may hold values from -6 to 6
- weight_in: bfloat16 [1024, 1024], P('feat'), may hold values from -0.1875 to 0.1875
- second_layer_weight: bfloat16 [1024, 1024], replicated, may hold values from -0.1875 to 0.1875
- send_rows: int32 [32, 32, 128], P('node'), may hold values from 0 to 1535
- recv_rows: int32 [32, 32, 128], P('node'), may hold values from 0 to 1535
- block_count: int32 [32, 32, 1], P('node'), may hold values from 16 to 128, as said below
Outputs:
- layer_two: bfloat16 [49152, 1024], P('node', 'feat')
The draws below stay inside these ranges and needn't reach their ends.
Inputs may be any that keep to these rules, and one draw needn't show every extreme that they name: `block_count`: blocks from partition q to partition p hold their live rows first; the most live rows in a block is 128.
All inputs are finite; a program needn't handle non-finite values.
Results may differ from the reference program's by a relative error of at most 0.025.
Values may be sent and summed in bfloat16 or wider, within the bound.
A program may use at most 64 MiB of HBM per device.

```python
import jax
import jax.numpy as jnp
from jax import lax

F = 1024
H = 1024
RDEV = 1536
BLK = 128
NB = 1
CAP = 128
NODES = 49152
N_NODE = 32
N_FEAT = 8


def draw_block_count(key, part):
    key = jax.random.fold_in(key, 11)
    key_order, key_light, key_full = jax.random.split(key, 3)
    shape = (N_NODE, N_NODE, NB)
    order = jax.random.permutation(key_order, N_NODE)
    heavy = (order % 4 == 0)[:, None, None]
    light = jax.random.randint(key_light, shape, BLK // 8, BLK // 2 + 1)
    full = jax.random.randint(key_full, shape, BLK // 2, BLK + 1)
    counts = jnp.where(heavy, full, light)
    busiest = jnp.argmin(order)
    counts = counts.at[busiest, 0, 0].set(BLK)
    return counts.astype(jnp.int32)


def set_ends(values, rng, least, high):
    extent = values.shape
    spot = [jax.random.randint(jax.random.fold_in(rng, axis), (), 0, extent[axis]) for axis in range(len(extent))]
    values = values.at[tuple(spot)].set(least)
    longest = extent.index(max(extent))
    spot[longest] = (spot[longest] + 1) % extent[longest]
    return values.at[tuple(spot)].set(high)


def levels(rng, shape, cuts, least, largest):
    factor_of, own = 1.0, jax.random.fold_in(rng, 6)
    for dim, blocks in cuts:
        draws = jnp.exp(jax.random.uniform(jax.random.fold_in(own, dim), (blocks,), jnp.float32, least / len(cuts), largest / len(cuts)))
        factor_of = factor_of * jnp.repeat(draws, shape[dim] // blocks).reshape([-1 if axis == dim else 1 for axis in range(len(shape))])
    return factor_of


def noise(own_key, extent, scale, most, pieces=(), kind=jnp.bfloat16):
    drawn = scale * jax.random.normal(own_key, extent, jnp.float32)
    if pieces:
        drawn = drawn * levels(own_key, extent, pieces, -0.22, 0.18)
    return jnp.clip(drawn, -most, most).astype(kind)


def setup_inputs(seed: int = 0) -> dict:
    splits = jax.random.split(jax.random.key(seed), 7)
    return {
        "batch_node_input": noise(splits[0], (NODES, F), 1.0, 6.0, ((0, 32), (1, 8))),
        "weight_in": noise(splits[1], (F, H), F ** -0.5, 0.1875, ((0, 8),)),
        "second_layer_weight": noise(splits[2], (H, H), H ** -0.5, 0.1875),
        "send_rows": set_ends(jax.random.randint(splits[3], (N_NODE, N_NODE, CAP), 0, RDEV), jax.random.fold_in(splits[3], 1), 0, RDEV - 1).astype(jnp.int32),
        "recv_rows": set_ends(jax.random.randint(splits[4], (N_NODE, N_NODE, CAP), 0, RDEV), jax.random.fold_in(splits[4], 1), 0, RDEV - 1).astype(jnp.int32),
        "block_count": draw_block_count(jax.random.fold_in(splits[6], 71), 0),
    }


def slice_product(left, right, parts):
    width = left.shape[1] // parts
    total = jnp.zeros((left.shape[0], right.shape[1]), jnp.float32)
    for which in range(parts):
        partial_value = jnp.dot(left[:, which * width:(which + 1) * width], right[which * width:(which + 1) * width], preferred_element_type=jnp.float32)
        total = total + lax.optimization_barrier(partial_value.astype(jnp.bfloat16)).astype(jnp.float32)
    return total


def edge_lists(send_rows, recv_rows, block_count):
    count = N_NODE
    slots = NB * BLK
    source = jnp.arange(count, dtype=jnp.int32)[None, :, None] * RDEV + jnp.transpose(send_rows, (1, 0, 2)).astype(jnp.int32)
    target_nodes = jnp.arange(count, dtype=jnp.int32)[:, None, None] * RDEV + recv_rows.astype(jnp.int32)
    live = (jnp.arange(BLK, dtype=jnp.int32)[None, None, None, :] < block_count[..., None]).reshape(count, count, slots).astype(jnp.float32)
    return source.reshape(-1), target_nodes.reshape(-1), live.reshape(-1)


def aggregate(dense_matrix, source, target_nodes, live, degree):
    moved = dense_matrix[source].astype(jnp.float32) * live[:, None]
    total = dense_matrix.astype(jnp.float32) + jax.ops.segment_sum(moved, target_nodes, num_segments=dense_matrix.shape[0])
    return total / degree[:, None]


def reference(batch_node_input, weight_in, second_layer_weight, send_rows, recv_rows, block_count):
    source, target_nodes, live = edge_lists(send_rows, recv_rows, block_count)
    degree = 1.0 + jax.ops.segment_sum(live, target_nodes, num_segments=batch_node_input.shape[0])
    first = slice_product(batch_node_input, weight_in, N_FEAT).astype(jnp.bfloat16)
    hidden = jnp.maximum(aggregate(first, source, target_nodes, live, degree), 0.0).astype(jnp.bfloat16)
    second = slice_product(hidden, second_layer_weight, N_FEAT).astype(jnp.bfloat16)
    return aggregate(second, source, target_nodes, live, degree).astype(jnp.bfloat16)
```

```python
import functools

import jax
import jax.numpy as jnp
from jax import lax
from jax.experimental import pallas as pl
from jax.experimental.pallas import tpu as pltpu
from jax.sharding import PartitionSpec as P

MESH = pl.DeviceIdType.MESH
NZ, NY, NX, NC = 8, 4, 4, 2
NODES, FEATS = NZ * NY, NX * NC
BF16, F32 = jnp.bfloat16, jnp.float32


def order(i):
    return lax.rem(4 + lax.rem(i, 2) * ((i + 1) // 2) - (1 - lax.rem(i, 2)) * (i // 2), NZ)


def kernel(
    x_ref, w1_ref, w2_hbm, send_ref, recv_ref, count_ref, out_ref,
    w1_all, w2_all, out_slots, in_slots, send_cols, recv_live, pick, place,
    total, degree, mine, rows_in, rows_out, second,
    slot_send, slot_recv, w1_send, w1_recv, w1_send2, w1_recv2, row_send, row_recv, w2_sem,
):
    rows, width = x_ref.shape
    slots = send_ref.shape[1]
    part = rows // FEATS
    node, feat = lax.axis_index("node"), lax.axis_index("feat")
    z, y = node // NY, lax.rem(node, NY)
    x, c = feat // NC, lax.rem(feat, NC)

    barrier = pltpu.get_barrier_semaphore()

    def greet_node(k, _):
        other = lax.rem(node + k, NODES)
        pl.semaphore_signal(barrier, inc=1, device_id=(other, feat), device_id_type=MESH)
        return 0

    def greet_feat(k, _):
        other = lax.rem(feat + k, FEATS)
        pl.semaphore_signal(barrier, inc=1, device_id=(node, other), device_id_type=MESH)
        return 0

    lax.fori_loop(1, FEATS, greet_feat, 0)
    lax.fori_loop(1, NODES, greet_node, 0)

    w2_copy = pltpu.make_async_copy(w2_hbm, w2_all, w2_sem)
    w2_copy.start()
    send_cols[...] = send_ref[...].astype(F32).T
    slot_id = lax.broadcasted_iota(jnp.int32, recv_ref.shape, 1)
    live = jnp.where(slot_id < count_ref[...], recv_ref[...], -1)
    for q in range(NZ):
        recv_live[q] = live[q * NY:(q + 1) * NY]
    w1_all[feat] = w1_ref[...]

    pl.semaphore_wait(barrier, NODES + FEATS - 2)

    def w1_copy(dx):
        return pltpu.make_async_remote_copy(
            w1_ref, w1_all.at[feat], w1_send.at[dx], w1_recv.at[dx],
            device_id=(node, lax.rem(x + dx, NX) * NC + c), device_id_type=MESH)

    def w1_pass(dx):
        held = lax.rem(x + NX - dx, NX) * NC + c
        return pltpu.make_async_remote_copy(
            w1_all.at[held], w1_all.at[held], w1_send2.at[dx], w1_recv2.at[dx],
            device_id=(node, x * NC + 1 - c), device_id_type=MESH)

    def slot_copy(layer, other):
        return pltpu.make_async_remote_copy(
            out_slots.at[layer, other], in_slots.at[layer, node],
            slot_send.at[layer, other], slot_recv.at[layer, node],
            device_id=(other, feat), device_id_type=MESH)

    def slot_wait(layer, other):
        pltpu.make_async_remote_copy(
            out_slots.at[layer, other], in_slots.at[layer, other],
            slot_send.at[layer, other], slot_recv.at[layer, other],
            device_id=(other, feat), device_id_type=MESH).wait_recv()

    def select(layer, source, zz):
        cols = send_cols[...]
        lane = lax.broadcasted_iota(jnp.int32, cols.shape, 1)
        row_id = lax.broadcasted_iota(jnp.int32, (slots, rows), 1).astype(F32)
        for j in range(NY):
            col = jnp.sum(jnp.where(lane == zz * NY + j, cols, 0.0), axis=1, keepdims=True)
            pick[j * slots:(j + 1) * slots, :] = jnp.where(row_id == col, 1.0, 0.0).astype(BF16)
        got = jnp.dot(pick[...], source[...], preferred_element_type=F32).astype(BF16)
        out_slots[layer, pl.ds(zz * NY, NY)] = got.reshape(NY, slots, width)

    def send_all(layer, source):
        def plane(i, _):
            zz = lax.rem(z + order(i), NZ)
            select(layer, source, zz)
            for j in range(NY):
                slot_copy(layer, zz * NY + j).start()
            return 0

        lax.fori_loop(0, NZ - 1, plane, 0)
        select(layer, source, z)
        for j in range(1, NY):
            slot_copy(layer, z * NY + lax.rem(y + j, NY)).start()
        in_slots[layer, node] = out_slots[layer, node]

    def add_plane(layer, zz):
        ids = recv_live[zz]
        row_id = lax.broadcasted_iota(jnp.int32, (rows, slots), 0)
        for j in range(NY):
            place[:, j * slots:(j + 1) * slots] = jnp.where(
                row_id == ids[j:j + 1, :], 1.0, 0.0).astype(BF16)
        held = in_slots[layer, pl.ds(zz * NY, NY)].reshape(NY * slots, width)
        if layer == 0:
            held = jnp.concatenate([held, jnp.ones_like(held)], axis=1)
            both = jnp.dot(place[...], held, preferred_element_type=F32)
            total[...] += both[:, :width]
            degree[...] += both[:, width:]
        else:
            total[...] += jnp.dot(place[...], held, preferred_element_type=F32)

    def add_all(layer, middle=None):
        for j in range(1, NY):
            slot_wait(layer, z * NY + lax.rem(y + j, NY))
        add_plane(layer, z)

        def plane(i, _):
            zz = lax.rem(z + NZ - order(NZ - 2 - i), NZ)
            for j in range(NY):
                slot_wait(layer, zz * NY + j)
            add_plane(layer, zz)
            return 0

        if middle is None:
            lax.fori_loop(0, NZ - 1, plane, 0)
        else:
            lax.fori_loop(0, NZ - 3, plane, 0)
            middle()
            lax.fori_loop(NZ - 3, NZ - 1, plane, 0)

    def pass_w1():
        for dx in range(1, NX):
            w1_copy(dx).wait_recv()
            w1_pass(dx).start()

    for dx in range(1, NX):
        w1_copy(dx).start()
    w1_pass(0).start()

    send_all(0, x_ref)
    total[...] = x_ref[...].astype(F32)
    degree[...] = jnp.ones_like(degree)
    add_all(0, pass_w1)
    mine[...] = (total[...] / degree[...]).astype(BF16)

    def row_copy(step, d):
        other = lax.rem(feat + d, FEATS)
        if step == 0:
            source = mine.at[pl.ds(pl.multiple_of(other * part, 16), part)]
            target = rows_in.at[feat]
        else:
            source = rows_out.at[other]
            target = second.at[pl.ds(pl.multiple_of(feat * part, 16), part)]
        return pltpu.make_async_remote_copy(
            source, target, row_send.at[step, d], row_recv.at[step, d],
            device_id=(node, other), device_id_type=MESH)

    for d in range(1, FEATS):
        row_copy(0, d).start()
    rows_in[feat] = mine[pl.ds(pl.multiple_of(feat * part, 16), part)]
    for dx in range(NX):
        w1_pass(dx).wait_recv()
    w2_copy.wait()
    for d in range(1, FEATS):
        row_copy(0, d).wait_recv()

    held = jnp.concatenate([rows_in[f] for f in range(FEATS)], axis=1)
    hidden = jnp.dot(held, w1_all[...].reshape(FEATS * width, FEATS * width), preferred_element_type=F32)
    hidden = jnp.maximum(hidden, 0.0).astype(BF16)
    result = jnp.dot(hidden, w2_all[...], preferred_element_type=F32).astype(BF16)
    for f in range(FEATS):
        rows_out[f] = result[:, f * width:(f + 1) * width]
    for d in range(1, FEATS):
        row_copy(1, d).start()
    second[pl.ds(pl.multiple_of(feat * part, 16), part)] = rows_out[feat]
    for d in range(1, FEATS):
        row_copy(1, d).wait_recv()

    send_all(1, second)
    total[...] = second[...].astype(F32)
    add_all(1)
    out_ref[...] = (total[...] / degree[...]).astype(BF16)

    def sent(k, _):
        other = lax.rem(node + k, NODES)
        slot_copy(0, other).wait_send()
        slot_copy(1, other).wait_send()
        return 0

    lax.fori_loop(1, NODES, sent, 0)
    for dx in range(1, NX):
        w1_copy(dx).wait_send()
    for dx in range(NX):
        w1_pass(dx).wait_send()
    for d in range(1, FEATS):
        row_copy(0, d).wait_send()
        row_copy(1, d).wait_send()


def per_device(batch_node_input, weight_in, second_layer_weight, send_rows, recv_rows, block_count):
    rows, width = batch_node_input.shape
    nodes, slots = send_rows.shape[1:]
    part = rows // FEATS
    hidden = weight_in.shape[1]
    vmem = pl.BlockSpec(memory_space=pltpu.VMEM)
    dma = pltpu.SemaphoreType.DMA
    return pl.pallas_call(
        kernel,
        out_shape=jax.ShapeDtypeStruct((rows, width), BF16),
        in_specs=[vmem, vmem, pl.BlockSpec(memory_space=pl.ANY), vmem, vmem, vmem],
        out_specs=vmem,
        scratch_shapes=[
            pltpu.VMEM((FEATS, width, hidden), BF16),
            pltpu.VMEM((hidden, hidden), BF16),
            pltpu.VMEM((2, nodes, slots, width), BF16),
            pltpu.VMEM((2, nodes, slots, width), BF16),
            pltpu.VMEM((slots, nodes), F32),
            pltpu.VMEM((NZ, NY, slots), jnp.int32),
            pltpu.VMEM((NY * slots, rows), BF16),
            pltpu.VMEM((rows, NY * slots), BF16),
            pltpu.VMEM((rows, width), F32),
            pltpu.VMEM((rows, width), F32),
            pltpu.VMEM((rows, width), BF16),
            pltpu.VMEM((FEATS, part, width), BF16),
            pltpu.VMEM((FEATS, part, width), BF16),
            pltpu.VMEM((rows, width), BF16),
            dma((2, nodes)), dma((2, nodes)),
            dma((NX,)), dma((NX,)), dma((NX,)), dma((NX,)),
            dma((2, FEATS)), dma((2, FEATS)),
            dma,
        ],
        compiler_params=pltpu.CompilerParams(
            collective_id=0, has_side_effects=True, vmem_limit_bytes=48 * 2**20),
    )(batch_node_input, weight_in, second_layer_weight, send_rows[0], recv_rows[0], block_count[0])


def solution(mesh):
    return jax.shard_map(
        per_device, mesh=mesh,
        in_specs=(P("node", "feat"), P("feat", None), P(), P("node", None, None), P("node", None, None), P("node", None, None)),
        out_specs=P("node", "feat"), check_vma=False)
```

```python
import functools

import jax
import jax.numpy as jnp
from jax import lax
from jax.experimental import pallas as pl
from jax.experimental.pallas import tpu as pltpu
from jax.sharding import PartitionSpec as P

MESH = pl.DeviceIdType.MESH
NZ, NY, NX, NC = 8, 4, 4, 2
NODES, FEATS = NZ * NY, NX * NC
BF16, F32 = jnp.bfloat16, jnp.float32


def order(i):
    return lax.rem(4 + lax.rem(i, 2) * ((i + 1) // 2) - (1 - lax.rem(i, 2)) * (i // 2), NZ)


def kernel(
    x_hbm, w1_hbm, w2_hbm, send_hbm, recv_hbm, count_hbm, out_ref,
    x_ref, send_ref, recv_ref, count_ref, w1_all, w2_all, out_slots, in_slots, send_cols, recv_live, pick, place,
    total, degree, mine, rows_in, rows_out, second,
    slot_send, slot_recv, w1_send, w1_recv, w1_send2, w1_recv2, row_send, row_recv, in_sem,
):
    rows, width = x_ref.shape
    slots = send_ref.shape[1]
    part = rows // FEATS
    node, feat = lax.axis_index("node"), lax.axis_index("feat")
    z, y = node // NY, lax.rem(node, NY)
    x, c = feat // NC, lax.rem(feat, NC)

    barrier = pltpu.get_barrier_semaphore()

    def greet_plane(i, _):
        zz = lax.rem(z + order(i), NZ)
        for j in range(NY):
            pl.semaphore_signal(barrier, inc=1, device_id=(zz * NY + j, feat), device_id_type=MESH)
        return 0

    lax.fori_loop(0, NZ - 1, greet_plane, 0)
    for j in range(1, NY):
        pl.semaphore_signal(
            barrier, inc=1, device_id=(z * NY + lax.rem(y + j, NY), feat), device_id_type=MESH)
    for d in range(1, FEATS):
        pl.semaphore_signal(
            barrier, inc=1, device_id=(node, lax.rem(feat + d, FEATS)), device_id_type=MESH)

    send_in = pltpu.make_async_copy(send_hbm, send_ref, in_sem.at[0])
    x_in = pltpu.make_async_copy(x_hbm, x_ref, in_sem.at[1])
    recv_in = pltpu.make_async_copy(recv_hbm, recv_ref, in_sem.at[2])
    count_in = pltpu.make_async_copy(count_hbm, count_ref, in_sem.at[3])
    w1_in = pltpu.make_async_copy(w1_hbm, w1_all.at[feat], in_sem.at[4])
    w2_in = pltpu.make_async_copy(w2_hbm, w2_all, in_sem.at[5])
    for copy in (send_in, x_in, recv_in, count_in, w1_in, w2_in):
        copy.start()

    def w1_copy(dx):
        return pltpu.make_async_remote_copy(
            w1_hbm, w1_all.at[feat], w1_send.at[dx], w1_recv.at[dx],
            device_id=(node, lax.rem(x + dx, NX) * NC + c), device_id_type=MESH)

    def w1_pass(dx):
        held = lax.rem(x + NX - dx, NX) * NC + c
        return pltpu.make_async_remote_copy(
            w1_hbm if dx == 0 else w1_all.at[held], w1_all.at[held], w1_send2.at[dx], w1_recv2.at[dx],
            device_id=(node, x * NC + 1 - c), device_id_type=MESH)

    def slot_copy(layer, other):
        return pltpu.make_async_remote_copy(
            out_slots.at[layer, other], in_slots.at[layer, node],
            slot_send.at[layer, other], slot_recv.at[layer, node],
            device_id=(other, feat), device_id_type=MESH)

    def slot_wait(layer, other):
        pltpu.make_async_remote_copy(
            out_slots.at[layer, other], in_slots.at[layer, other],
            slot_send.at[layer, other], slot_recv.at[layer, other],
            device_id=(other, feat), device_id_type=MESH).wait_recv()

    def build_pick(zz):
        cols = send_cols[...]
        lane = lax.broadcasted_iota(jnp.int32, cols.shape, 1)
        row_id = lax.broadcasted_iota(jnp.int32, (slots, rows), 1).astype(F32)
        for j in range(NY):
            col = jnp.sum(jnp.where(lane == zz * NY + j, cols, 0.0), axis=1, keepdims=True)
            pick[zz, j * slots:(j + 1) * slots, :] = jnp.where(row_id == col, 1.0, 0.0).astype(BF16)

    def select(layer, source, zz):
        if layer == 0:
            build_pick(zz)
        got = jnp.dot(pick[zz], source[...], preferred_element_type=F32).astype(BF16)
        out_slots[layer, pl.ds(zz * NY, NY)] = got.reshape(NY, slots, width)

    def send_plane(layer, zz):
        for j in range(NY):
            slot_copy(layer, zz * NY + j).start()

    def far(i):
        return lax.rem(z + order(i), NZ)

    def send_rest(layer, source, first):
        def plane(i, _):
            select(layer, source, far(i))
            send_plane(layer, far(i))
            return 0

        lax.fori_loop(first, NZ - 1, plane, 0)
        select(layer, source, z)
        for j in range(1, NY):
            slot_copy(layer, z * NY + lax.rem(y + j, NY)).start()
        in_slots[layer, node] = out_slots[layer, node]

    def build_place(zz, _):
        ids = recv_live[zz]
        row_id = lax.broadcasted_iota(jnp.int32, (rows, slots), 0)
        for j in range(NY):
            place[zz, :, j * slots:(j + 1) * slots] = jnp.where(
                row_id == ids[j:j + 1, :], 1.0, 0.0).astype(BF16)
        return 0

    def add_plane(layer, zz):
        held = in_slots[layer, pl.ds(zz * NY, NY)].reshape(NY * slots, width)
        if layer == 0:
            held = jnp.concatenate([held, jnp.ones_like(held)], axis=1)
            both = jnp.dot(place[zz], held, preferred_element_type=F32)
            total[...] += both[:, :width]
            degree[...] += both[:, width:]
        else:
            total[...] += jnp.dot(place[zz], held, preferred_element_type=F32)

    def add_all(layer, middle=None):
        for j in range(1, NY):
            slot_wait(layer, z * NY + lax.rem(y + j, NY))
        add_plane(layer, z)

        def plane(i, _):
            zz = lax.rem(z + NZ - order(NZ - 2 - i), NZ)
            for j in range(NY):
                slot_wait(layer, zz * NY + j)
            add_plane(layer, zz)
            return 0

        if middle is None:
            lax.fori_loop(0, NZ - 1, plane, 0)
        else:
            lax.fori_loop(0, NZ - 3, plane, 0)
            middle()
            lax.fori_loop(NZ - 3, NZ - 1, plane, 0)

    def pass_w1():
        for dx in range(1, NX):
            w1_copy(dx).wait_recv()
            w1_pass(dx).start()

    early = 2
    send_in.wait()
    send_cols[...] = send_ref[...].astype(F32).T
    x_in.wait()
    for i in range(early):
        select(0, x_ref, far(i))

    pl.semaphore_wait(barrier, NODES + FEATS - 2)

    for i in range(early):
        send_plane(0, far(i))
    for dx in range(1, NX):
        w1_copy(dx).start()
    w1_pass(0).start()

    send_rest(0, x_ref, early)

    recv_in.wait()
    count_in.wait()
    nodes = recv_ref.shape[0]
    across = (lax.broadcasted_iota(jnp.int32, (nodes, nodes), 0)
              == lax.broadcasted_iota(jnp.int32, (nodes, nodes), 1))
    counts = jnp.sum(jnp.where(across, count_ref[...].astype(F32), 0.0), axis=1, keepdims=True)
    slot_id = lax.broadcasted_iota(jnp.int32, recv_ref.shape, 1).astype(F32)
    live = jnp.where(slot_id < counts, recv_ref[...], -1)
    for q in range(NZ):
        recv_live[q] = live[q * NY:(q + 1) * NY]
    lax.fori_loop(0, NZ, build_place, 0)

    total[...] = x_ref[...].astype(F32)
    degree[...] = jnp.ones_like(degree)
    add_all(0, pass_w1)
    degree[...] = 1.0 / degree[...]
    mine[...] = (total[...] * degree[...]).astype(BF16)

    def row_copy(step, d):
        other = lax.rem(feat + d, FEATS)
        if step == 0:
            source = mine.at[pl.ds(pl.multiple_of(other * part, 16), part)]
            target = rows_in.at[feat]
        else:
            source = rows_out.at[other]
            target = second.at[pl.ds(pl.multiple_of(feat * part, 16), part)]
        return pltpu.make_async_remote_copy(
            source, target, row_send.at[step, d], row_recv.at[step, d],
            device_id=(node, other), device_id_type=MESH)

    for d in range(1, FEATS):
        row_copy(0, d).start()
    rows_in[feat] = mine[pl.ds(pl.multiple_of(feat * part, 16), part)]
    for dx in range(NX):
        w1_pass(dx).wait_recv()
    w1_in.wait()
    w2_in.wait()
    for d in range(1, FEATS):
        row_copy(0, d).wait_recv()

    held = jnp.concatenate([rows_in[f] for f in range(FEATS)], axis=1)
    hidden = jnp.dot(held, w1_all[...].reshape(FEATS * width, FEATS * width), preferred_element_type=F32)
    hidden = jnp.maximum(hidden, 0.0).astype(BF16)
    result = jnp.dot(hidden, w2_all[...], preferred_element_type=F32).astype(BF16)
    for f in range(FEATS):
        rows_out[f] = result[:, f * width:(f + 1) * width]
    for d in range(1, FEATS):
        row_copy(1, d).start()
    second[pl.ds(pl.multiple_of(feat * part, 16), part)] = rows_out[feat]
    for d in range(1, FEATS):
        row_copy(1, d).wait_recv()

    send_rest(1, second, 0)
    total[...] = second[...].astype(F32)
    add_all(1)
    out_ref[...] = (total[...] * degree[...]).astype(BF16)

    def sent(k, _):
        other = lax.rem(node + k, NODES)
        slot_copy(0, other).wait_send()
        slot_copy(1, other).wait_send()
        return 0

    lax.fori_loop(1, NODES, sent, 0)
    for dx in range(1, NX):
        w1_copy(dx).wait_send()
    for dx in range(NX):
        w1_pass(dx).wait_send()
    for d in range(1, FEATS):
        row_copy(0, d).wait_send()
        row_copy(1, d).wait_send()


def per_device(batch_node_input, weight_in, second_layer_weight, send_rows, recv_rows, block_count):
    rows, width = batch_node_input.shape
    nodes, slots = send_rows.shape[1:]
    part = rows // FEATS
    hidden = weight_in.shape[1]
    vmem = pl.BlockSpec(memory_space=pltpu.VMEM)
    dma = pltpu.SemaphoreType.DMA
    return pl.pallas_call(
        kernel,
        out_shape=jax.ShapeDtypeStruct((rows, width), BF16),
        in_specs=[pl.BlockSpec(memory_space=pltpu.HBM)] * 6,
        out_specs=vmem,
        scratch_shapes=[
            pltpu.VMEM((rows, width), BF16),
            pltpu.VMEM((nodes, slots), jnp.int32),
            pltpu.VMEM((nodes, slots), jnp.int32),
            pltpu.VMEM((1, nodes), jnp.int32),
            pltpu.VMEM((FEATS, width, hidden), BF16),
            pltpu.VMEM((hidden, hidden), BF16),
            pltpu.VMEM((2, nodes, slots, width), BF16),
            pltpu.VMEM((2, nodes, slots, width), BF16),
            pltpu.VMEM((slots, nodes), F32),
            pltpu.VMEM((NZ, NY, slots), jnp.int32),
            pltpu.VMEM((NZ, NY * slots, rows), BF16),
            pltpu.VMEM((NZ, rows, NY * slots), BF16),
            pltpu.VMEM((rows, width), F32),
            pltpu.VMEM((rows, width), F32),
            pltpu.VMEM((rows, width), BF16),
            pltpu.VMEM((FEATS, part, width), BF16),
            pltpu.VMEM((FEATS, part, width), BF16),
            pltpu.VMEM((rows, width), BF16),
            dma((2, nodes)), dma((2, nodes)),
            dma((NX,)), dma((NX,)), dma((NX,)), dma((NX,)),
            dma((2, FEATS)), dma((2, FEATS)),
            dma((6,)),
        ],
        compiler_params=pltpu.CompilerParams(
            collective_id=0, has_side_effects=True, vmem_limit_bytes=60 * 2**20),
    )(batch_node_input, weight_in, second_layer_weight, send_rows[0], recv_rows[0], block_count[:, :, 0])


def solution(mesh):
    return jax.shard_map(
        per_device, mesh=mesh,
        in_specs=(P("node", "feat"), P("feat", None), P(), P("node", None, None), P("node", None, None), P("node", None, None)),
        out_specs=P("node", "feat"), check_vma=False)
```

```python
import functools

import jax
import jax.numpy as jnp
from jax import lax
from jax.experimental import pallas as pl
from jax.experimental.pallas import tpu as pltpu
from jax.sharding import PartitionSpec as P

MESH = pl.DeviceIdType.MESH
NZ, NY, NX, NC = 8, 4, 4, 2
NODES, FEATS = NZ * NY, NX * NC
BF16, F32 = jnp.bfloat16, jnp.float32


def order(i):
    return lax.rem(4 + lax.rem(i, 2) * ((i + 1) // 2) - (1 - lax.rem(i, 2)) * (i // 2), NZ)


def kernel(
    x_hbm, w1_hbm, w2_hbm, send_hbm, recv_hbm, count_hbm, out_ref,
    x_ref, send_ref, recv_ref, count_ref, w1_all, w2_all, out_slots, in_slots, send_cols, recv_live, pick, place,
    total, degree, mine, rows_in, rows_out, second,
    slot_send, slot_recv, w1_send, w1_recv, w1_send2, w1_recv2, row_send, row_recv, in_sem,
):
    rows, width = x_ref.shape
    slots = send_ref.shape[1]
    part = rows // FEATS
    node, feat = lax.axis_index("node"), lax.axis_index("feat")
    z, y = node // NY, lax.rem(node, NY)
    x, c = feat // NC, lax.rem(feat, NC)

    barrier = pltpu.get_barrier_semaphore()

    def greet_plane(i, _):
        zz = lax.rem(z + order(i), NZ)
        for j in range(NY):
            pl.semaphore_signal(barrier, inc=1, device_id=(zz * NY + j, feat), device_id_type=MESH)
        return 0

    lax.fori_loop(0, NZ - 1, greet_plane, 0)
    for j in range(1, NY):
        pl.semaphore_signal(
            barrier, inc=1, device_id=(z * NY + lax.rem(y + j, NY), feat), device_id_type=MESH)
    for d in range(1, FEATS):
        pl.semaphore_signal(
            barrier, inc=1, device_id=(node, lax.rem(feat + d, FEATS)), device_id_type=MESH)

    send_in = pltpu.make_async_copy(send_hbm, send_ref, in_sem.at[0])
    x_in = pltpu.make_async_copy(x_hbm, x_ref, in_sem.at[1])
    recv_in = pltpu.make_async_copy(recv_hbm, recv_ref, in_sem.at[2])
    count_in = pltpu.make_async_copy(count_hbm, count_ref, in_sem.at[3])
    w1_in = pltpu.make_async_copy(w1_hbm, w1_all.at[feat], in_sem.at[4])
    w2_in = pltpu.make_async_copy(w2_hbm, w2_all, in_sem.at[5])
    for copy in (send_in, x_in, recv_in, count_in, w1_in, w2_in):
        copy.start()

    def w1_copy(dx):
        return pltpu.make_async_remote_copy(
            w1_hbm, w1_all.at[feat], w1_send.at[dx], w1_recv.at[dx],
            device_id=(node, lax.rem(x + dx, NX) * NC + c), device_id_type=MESH)

    def w1_pass(dx):
        held = lax.rem(x + NX - dx, NX) * NC + c
        return pltpu.make_async_remote_copy(
            w1_hbm if dx == 0 else w1_all.at[held], w1_all.at[held], w1_send2.at[dx], w1_recv2.at[dx],
            device_id=(node, x * NC + 1 - c), device_id_type=MESH)

    def slot_copy(layer, other):
        return pltpu.make_async_remote_copy(
            out_slots.at[layer, other], in_slots.at[layer, node],
            slot_send.at[layer, other], slot_recv.at[layer, node],
            device_id=(other, feat), device_id_type=MESH)

    def slot_wait(layer, other):
        pltpu.make_async_remote_copy(
            out_slots.at[layer, other], in_slots.at[layer, other],
            slot_send.at[layer, other], slot_recv.at[layer, other],
            device_id=(other, feat), device_id_type=MESH).wait_recv()

    def build_pick(zz):
        cols = send_cols[...]
        lane = lax.broadcasted_iota(jnp.int32, cols.shape, 1)
        row_id = lax.broadcasted_iota(jnp.int32, (slots, rows), 1).astype(F32)
        for j in range(NY):
            col = jnp.sum(jnp.where(lane == zz * NY + j, cols, 0.0), axis=1, keepdims=True)
            pick[zz, j * slots:(j + 1) * slots, :] = jnp.where(row_id == col, 1.0, 0.0).astype(BF16)

    def select(layer, source, zz):
        if layer == 0:
            build_pick(zz)
        got = jnp.dot(pick[zz], source[...], preferred_element_type=F32).astype(BF16)
        out_slots[layer, pl.ds(zz * NY, NY)] = got.reshape(NY, slots, width)

    def send_plane(layer, zz):
        for j in range(NY):
            slot_copy(layer, zz * NY + j).start()

    def near(i):
        return lax.rem(z + order(NZ - 2 - i), NZ)

    def send_rest(layer, source, first):
        def plane(i, _):
            select(layer, source, near(i))
            send_plane(layer, near(i))
            return 0

        lax.fori_loop(first, NZ - 1, plane, 0)
        select(layer, source, z)
        for j in range(1, NY):
            slot_copy(layer, z * NY + lax.rem(y + j, NY)).start()
        in_slots[layer, node] = out_slots[layer, node]

    def build_place(zz, _):
        ids = recv_live[zz]
        row_id = lax.broadcasted_iota(jnp.int32, (rows, slots), 0)
        for j in range(NY):
            place[zz, :, j * slots:(j + 1) * slots] = jnp.where(
                row_id == ids[j:j + 1, :], 1.0, 0.0).astype(BF16)
        return 0

    def add_plane(layer, zz):
        held = in_slots[layer, pl.ds(zz * NY, NY)].reshape(NY * slots, width)
        if layer == 0:
            held = jnp.concatenate([held, jnp.ones_like(held)], axis=1)
            both = jnp.dot(place[zz], held, preferred_element_type=F32)
            total[...] += both[:, :width]
            degree[...] += both[:, width:]
        else:
            total[...] += jnp.dot(place[zz], held, preferred_element_type=F32)

    def add_all(layer, middle=None):
        for j in range(1, NY):
            slot_wait(layer, z * NY + lax.rem(y + j, NY))
        add_plane(layer, z)

        def plane(i, _):
            zz = lax.rem(z + NZ - order(NZ - 2 - i), NZ)
            for j in range(NY):
                slot_wait(layer, zz * NY + j)
            add_plane(layer, zz)
            return 0

        if middle is None:
            lax.fori_loop(0, NZ - 1, plane, 0)
        else:
            lax.fori_loop(0, NZ - 3, plane, 0)
            middle()
            lax.fori_loop(NZ - 3, NZ - 1, plane, 0)

    def pass_w1():
        for dx in range(1, NX):
            w1_copy(dx).wait_recv()
            w1_pass(dx).start()

    early = 2
    send_in.wait()
    send_cols[...] = send_ref[...].astype(F32).T
    x_in.wait()
    for i in range(early):
        select(0, x_ref, near(i))

    pl.semaphore_wait(barrier, NODES + FEATS - 2)

    for i in range(early):
        send_plane(0, near(i))
    for dx in range(1, NX):
        w1_copy(dx).start()
    w1_pass(0).start()

    send_rest(0, x_ref, early)

    recv_in.wait()
    count_in.wait()
    nodes = recv_ref.shape[0]
    across = (lax.broadcasted_iota(jnp.int32, (nodes, nodes), 0)
              == lax.broadcasted_iota(jnp.int32, (nodes, nodes), 1))
    counts = jnp.sum(jnp.where(across, count_ref[...].astype(F32), 0.0), axis=1, keepdims=True)
    slot_id = lax.broadcasted_iota(jnp.int32, recv_ref.shape, 1).astype(F32)
    live = jnp.where(slot_id < counts, recv_ref[...], -1)
    for q in range(NZ):
        recv_live[q] = live[q * NY:(q + 1) * NY]
    lax.fori_loop(0, NZ, build_place, 0)

    total[...] = x_ref[...].astype(F32)
    degree[...] = jnp.ones_like(degree)
    add_all(0, pass_w1)
    degree[...] = 1.0 / degree[...]
    mine[...] = (total[...] * degree[...]).astype(BF16)

    def row_copy(step, d):
        other = lax.rem(feat + d, FEATS)
        if step == 0:
            source = mine.at[pl.ds(pl.multiple_of(other * part, 16), part)]
            target = rows_in.at[feat]
        else:
            source = rows_out.at[other]
            target = second.at[pl.ds(pl.multiple_of(feat * part, 16), part)]
        return pltpu.make_async_remote_copy(
            source, target, row_send.at[step, d], row_recv.at[step, d],
            device_id=(node, other), device_id_type=MESH)

    for d in range(1, FEATS):
        row_copy(0, d).start()
    rows_in[feat] = mine[pl.ds(pl.multiple_of(feat * part, 16), part)]
    for dx in range(NX):
        w1_pass(dx).wait_recv()
    w1_in.wait()
    w2_in.wait()
    for d in range(1, FEATS):
        row_copy(0, d).wait_recv()

    held = jnp.concatenate([rows_in[f] for f in range(FEATS)], axis=1)
    hidden = jnp.dot(held, w1_all[...].reshape(FEATS * width, FEATS * width), preferred_element_type=F32)
    hidden = jnp.maximum(hidden, 0.0).astype(BF16)
    result = jnp.dot(hidden, w2_all[...], preferred_element_type=F32).astype(BF16)
    for f in range(FEATS):
        rows_out[f] = result[:, f * width:(f + 1) * width]
    for d in range(1, FEATS):
        row_copy(1, d).start()
    second[pl.ds(pl.multiple_of(feat * part, 16), part)] = rows_out[feat]
    for d in range(1, FEATS):
        row_copy(1, d).wait_recv()

    send_rest(1, second, 0)
    total[...] = second[...].astype(F32)
    add_all(1)
    out_ref[...] = (total[...] * degree[...]).astype(BF16)

    def sent(k, _):
        other = lax.rem(node + k, NODES)
        slot_copy(0, other).wait_send()
        slot_copy(1, other).wait_send()
        return 0

    lax.fori_loop(1, NODES, sent, 0)
    for dx in range(1, NX):
        w1_copy(dx).wait_send()
    for dx in range(NX):
        w1_pass(dx).wait_send()
    for d in range(1, FEATS):
        row_copy(0, d).wait_send()
        row_copy(1, d).wait_send()


def per_device(batch_node_input, weight_in, second_layer_weight, send_rows, recv_rows, block_count):
    rows, width = batch_node_input.shape
    nodes, slots = send_rows.shape[1:]
    part = rows // FEATS
    hidden = weight_in.shape[1]
    vmem = pl.BlockSpec(memory_space=pltpu.VMEM)
    dma = pltpu.SemaphoreType.DMA
    return pl.pallas_call(
        kernel,
        out_shape=jax.ShapeDtypeStruct((rows, width), BF16),
        in_specs=[pl.BlockSpec(memory_space=pltpu.HBM)] * 6,
        out_specs=vmem,
        scratch_shapes=[
            pltpu.VMEM((rows, width), BF16),
            pltpu.VMEM((nodes, slots), jnp.int32),
            pltpu.VMEM((nodes, slots), jnp.int32),
            pltpu.VMEM((1, nodes), jnp.int32),
            pltpu.VMEM((FEATS, width, hidden), BF16),
            pltpu.VMEM((hidden, hidden), BF16),
            pltpu.VMEM((2, nodes, slots, width), BF16),
            pltpu.VMEM((2, nodes, slots, width), BF16),
            pltpu.VMEM((slots, nodes), F32),
            pltpu.VMEM((NZ, NY, slots), jnp.int32),
            pltpu.VMEM((NZ, NY * slots, rows), BF16),
            pltpu.VMEM((NZ, rows, NY * slots), BF16),
            pltpu.VMEM((rows, width), F32),
            pltpu.VMEM((rows, width), F32),
            pltpu.VMEM((rows, width), BF16),
            pltpu.VMEM((FEATS, part, width), BF16),
            pltpu.VMEM((FEATS, part, width), BF16),
            pltpu.VMEM((rows, width), BF16),
            dma((2, nodes)), dma((2, nodes)),
            dma((NX,)), dma((NX,)), dma((NX,)), dma((NX,)),
            dma((2, FEATS)), dma((2, FEATS)),
            dma((6,)),
        ],
        compiler_params=pltpu.CompilerParams(
            collective_id=0, has_side_effects=True, vmem_limit_bytes=44 * 2**20),
    )(batch_node_input, weight_in, second_layer_weight, send_rows[0], recv_rows[0], block_count[:, :, 0])


def solution(mesh):
    return jax.shard_map(
        per_device, mesh=mesh,
        in_specs=(P("node", "feat"), P("feat", None), P(), P("node", None, None), P("node", None, None), P("node", None, None)),
        out_specs=P("node", "feat"), check_vma=False)
```

```python
import functools

import jax
import jax.numpy as jnp
from jax import lax
from jax.experimental import pallas as pl
from jax.experimental.pallas import tpu as pltpu
from jax.sharding import PartitionSpec as P

MESH = pl.DeviceIdType.MESH
NZ, NY, NX, NC = 8, 4, 4, 2
NODES, FEATS = NZ * NY, NX * NC
PIECES = 2
FEAT_STEPS = ((2, 0), (2, 1), (1, 0), (3, 0), (1, 1), (3, 1), (0, 1))
BF16, F32 = jnp.bfloat16, jnp.float32


def order(i):
    return lax.rem(4 + lax.rem(i, 2) * ((i + 1) // 2) - (1 - lax.rem(i, 2)) * (i // 2), NZ)


def kernel(
    x_hbm, w1_hbm, w2_hbm, send_hbm, recv_hbm, count_hbm, out_ref,
    x_ref, send_ref, recv_ref, count_ref, w1_all, w2_all, out_slots, in_slots, send_cols, recv_live, pick, place,
    total, degree, mine, rows_in, rows_out, second,
    slot_send, slot_recv, w1_send, w1_recv, w1_send2, w1_recv2, row_send, row_recv, in_sem,
):
    rows, width = x_ref.shape
    slots = send_ref.shape[1]
    part = rows // FEATS
    node, feat = lax.axis_index("node"), lax.axis_index("feat")
    z, y = node // NY, lax.rem(node, NY)
    x, c = feat // NC, lax.rem(feat, NC)

    barrier = pltpu.get_barrier_semaphore()

    def greet_plane(i, _):
        zz = lax.rem(z + order(i), NZ)
        for j in range(NY):
            pl.semaphore_signal(barrier, inc=1, device_id=(zz * NY + j, feat), device_id_type=MESH)
        return 0

    lax.fori_loop(0, NZ - 1, greet_plane, 0)
    for j in range(1, NY):
        pl.semaphore_signal(
            barrier, inc=1, device_id=(z * NY + lax.rem(y + j, NY), feat), device_id_type=MESH)
    for d in range(1, FEATS):
        pl.semaphore_signal(
            barrier, inc=1, device_id=(node, lax.rem(feat + d, FEATS)), device_id_type=MESH)

    send_in = pltpu.make_async_copy(send_hbm, send_ref, in_sem.at[0])
    x_in = pltpu.make_async_copy(x_hbm, x_ref, in_sem.at[1])
    recv_in = pltpu.make_async_copy(recv_hbm, recv_ref, in_sem.at[2])
    count_in = pltpu.make_async_copy(count_hbm, count_ref, in_sem.at[3])
    w1_in = pltpu.make_async_copy(w1_hbm, w1_all.at[feat], in_sem.at[4])
    w2_in = pltpu.make_async_copy(w2_hbm, w2_all, in_sem.at[5])
    for copy in (send_in, x_in, recv_in, count_in, w1_in, w2_in):
        copy.start()

    def w1_copy(dx):
        return pltpu.make_async_remote_copy(
            w1_hbm, w1_all.at[feat], w1_send.at[dx], w1_recv.at[dx],
            device_id=(node, lax.rem(x + dx, NX) * NC + c), device_id_type=MESH)

    def w1_pass(dx):
        held = lax.rem(x + NX - dx, NX) * NC + c
        return pltpu.make_async_remote_copy(
            w1_hbm if dx == 0 else w1_all.at[held], w1_all.at[held], w1_send2.at[dx], w1_recv2.at[dx],
            device_id=(node, x * NC + 1 - c), device_id_type=MESH)

    def slot_copy(layer, other):
        return pltpu.make_async_remote_copy(
            out_slots.at[layer, other], in_slots.at[layer, node],
            slot_send.at[layer, other], slot_recv.at[layer, node],
            device_id=(other, feat), device_id_type=MESH)

    def slot_wait(layer, other):
        pltpu.make_async_remote_copy(
            out_slots.at[layer, other], in_slots.at[layer, other],
            slot_send.at[layer, other], slot_recv.at[layer, other],
            device_id=(other, feat), device_id_type=MESH).wait_recv()

    def build_pick(zz):
        cols = send_cols[...]
        lane = lax.broadcasted_iota(jnp.int32, cols.shape, 1)
        row_id = lax.broadcasted_iota(jnp.int32, (slots, rows), 1).astype(F32)
        for j in range(NY):
            col = jnp.sum(jnp.where(lane == zz * NY + j, cols, 0.0), axis=1, keepdims=True)
            pick[zz, j * slots:(j + 1) * slots, :] = jnp.where(row_id == col, 1.0, 0.0).astype(BF16)

    def select(layer, source, zz):
        if layer == 0:
            build_pick(zz)
        got = jnp.dot(pick[zz], source[...], preferred_element_type=F32).astype(BF16)
        out_slots[layer, pl.ds(zz * NY, NY)] = got.reshape(NY, slots, width)

    def send_plane(layer, zz):
        for j in range(NY):
            slot_copy(layer, zz * NY + j).start()

    def near(i):
        return lax.rem(z + order(NZ - 2 - i), NZ)

    def send_rest(layer, source, first):
        def plane(i, _):
            select(layer, source, near(i))
            send_plane(layer, near(i))
            return 0

        lax.fori_loop(first, NZ - 1, plane, 0)
        select(layer, source, z)
        for j in range(1, NY):
            slot_copy(layer, z * NY + lax.rem(y + j, NY)).start()
        in_slots[layer, node] = out_slots[layer, node]

    def build_place(zz, _):
        ids = recv_live[zz]
        row_id = lax.broadcasted_iota(jnp.int32, (rows, slots), 0)
        for j in range(NY):
            place[zz, :, j * slots:(j + 1) * slots] = jnp.where(
                row_id == ids[j:j + 1, :], 1.0, 0.0).astype(BF16)
        degree[...] += jnp.dot(
            place[zz], jnp.ones((NY * slots, width), BF16), preferred_element_type=F32)
        return 0

    def add_plane(layer, zz):
        held = in_slots[layer, pl.ds(zz * NY, NY)].reshape(NY * slots, width)
        total[...] += jnp.dot(place[zz], held, preferred_element_type=F32)

    def add_all(layer, middle=None):
        for j in range(1, NY):
            slot_wait(layer, z * NY + lax.rem(y + j, NY))
        add_plane(layer, z)

        def plane(i, _):
            zz = lax.rem(z + NZ - order(NZ - 2 - i), NZ)
            for j in range(NY):
                slot_wait(layer, zz * NY + j)
            add_plane(layer, zz)
            return 0

        if middle is None:
            lax.fori_loop(0, NZ - 1, plane, 0)
        else:
            lax.fori_loop(0, NZ - 3, plane, 0)
            middle()
            lax.fori_loop(NZ - 3, NZ - 1, plane, 0)

    def pass_w1():
        for dx in range(1, NX):
            w1_copy(dx).wait_recv()
            w1_pass(dx).start()

    early = 2
    send_in.wait()
    send_cols[...] = send_ref[...].astype(F32).T
    x_in.wait()
    for i in range(early):
        select(0, x_ref, near(i))

    pl.semaphore_wait(barrier, NODES + FEATS - 2)

    for i in range(early):
        send_plane(0, near(i))
    for dx in range(1, NX):
        w1_copy(dx).start()
    w1_pass(0).start()

    send_rest(0, x_ref, early)

    recv_in.wait()
    count_in.wait()
    nodes = recv_ref.shape[0]
    across = (lax.broadcasted_iota(jnp.int32, (nodes, nodes), 0)
              == lax.broadcasted_iota(jnp.int32, (nodes, nodes), 1))
    counts = jnp.sum(jnp.where(across, count_ref[...].astype(F32), 0.0), axis=1, keepdims=True)
    slot_id = lax.broadcasted_iota(jnp.int32, recv_ref.shape, 1).astype(F32)
    live = jnp.where(slot_id < counts, recv_ref[...], -1)
    for q in range(NZ):
        recv_live[q] = live[q * NY:(q + 1) * NY]
    degree[...] = jnp.ones_like(degree)
    lax.fori_loop(0, NZ, build_place, 0)
    degree[...] = 1.0 / degree[...]

    total[...] = x_ref[...].astype(F32)
    add_all(0, pass_w1)
    mine[...] = (total[...] * degree[...]).astype(BF16)

    piece = part // PIECES

    def row_copy(step, h, d):
        dx, dc = FEAT_STEPS[d]
        other = lax.rem(x + dx, NX) * NC + lax.rem(c + dc, NC)
        if step == 0:
            source = mine.at[pl.ds(pl.multiple_of(other * part + h * piece, 16), piece)]
            target = rows_in.at[feat, pl.ds(h * piece, piece)]
        else:
            source = rows_out.at[other, pl.ds(h * piece, piece)]
            target = second.at[pl.ds(pl.multiple_of(feat * part + h * piece, 16), piece)]
        return pltpu.make_async_remote_copy(
            source, target, row_send.at[step, h, d], row_recv.at[step, h, d],
            device_id=(node, other), device_id_type=MESH)

    each = range(len(FEAT_STEPS))
    for h in range(PIECES):
        for d in each:
            row_copy(0, h, d).start()
    rows_in[feat] = mine[pl.ds(pl.multiple_of(feat * part, 16), part)]
    for dx in range(NX):
        w1_pass(dx).wait_recv()
    w1_in.wait()
    w2_in.wait()
    for h in range(PIECES):
        for d in each:
            row_copy(0, h, d).wait_recv()
        held = jnp.concatenate([rows_in[f, h * piece:(h + 1) * piece] for f in range(FEATS)], axis=1)
        hidden = jnp.dot(
            held, w1_all[...].reshape(FEATS * width, FEATS * width), preferred_element_type=F32)
        hidden = jnp.maximum(hidden, 0.0).astype(BF16)
        result = jnp.dot(hidden, w2_all[...], preferred_element_type=F32).astype(BF16)
        for f in range(FEATS):
            rows_out[f, h * piece:(h + 1) * piece] = result[:, f * width:(f + 1) * width]
        for d in each:
            row_copy(1, h, d).start()
    second[pl.ds(pl.multiple_of(feat * part, 16), part)] = rows_out[feat]
    for h in range(PIECES):
        for d in each:
            row_copy(1, h, d).wait_recv()

    send_rest(1, second, 0)
    total[...] = second[...].astype(F32)
    add_all(1)
    out_ref[...] = (total[...] * degree[...]).astype(BF16)

    def sent(k, _):
        other = lax.rem(node + k, NODES)
        slot_copy(0, other).wait_send()
        slot_copy(1, other).wait_send()
        return 0

    lax.fori_loop(1, NODES, sent, 0)
    for dx in range(1, NX):
        w1_copy(dx).wait_send()
    for dx in range(NX):
        w1_pass(dx).wait_send()
    for h in range(PIECES):
        for d in each:
            row_copy(0, h, d).wait_send()
            row_copy(1, h, d).wait_send()


def per_device(batch_node_input, weight_in, second_layer_weight, send_rows, recv_rows, block_count):
    rows, width = batch_node_input.shape
    nodes, slots = send_rows.shape[1:]
    part = rows // FEATS
    hidden = weight_in.shape[1]
    vmem = pl.BlockSpec(memory_space=pltpu.VMEM)
    dma = pltpu.SemaphoreType.DMA
    return pl.pallas_call(
        kernel,
        out_shape=jax.ShapeDtypeStruct((rows, width), BF16),
        in_specs=[pl.BlockSpec(memory_space=pltpu.HBM)] * 6,
        out_specs=vmem,
        scratch_shapes=[
            pltpu.VMEM((rows, width), BF16),
            pltpu.VMEM((nodes, slots), jnp.int32),
            pltpu.VMEM((nodes, slots), jnp.int32),
            pltpu.VMEM((1, nodes), jnp.int32),
            pltpu.VMEM((FEATS, width, hidden), BF16),
            pltpu.VMEM((hidden, hidden), BF16),
            pltpu.VMEM((2, nodes, slots, width), BF16),
            pltpu.VMEM((2, nodes, slots, width), BF16),
            pltpu.VMEM((slots, nodes), F32),
            pltpu.VMEM((NZ, NY, slots), jnp.int32),
            pltpu.VMEM((NZ, NY * slots, rows), BF16),
            pltpu.VMEM((NZ, rows, NY * slots), BF16),
            pltpu.VMEM((rows, width), F32),
            pltpu.VMEM((rows, width), F32),
            pltpu.VMEM((rows, width), BF16),
            pltpu.VMEM((FEATS, part, width), BF16),
            pltpu.VMEM((FEATS, part, width), BF16),
            pltpu.VMEM((rows, width), BF16),
            dma((2, nodes)), dma((2, nodes)),
            dma((NX,)), dma((NX,)), dma((NX,)), dma((NX,)),
            dma((2, PIECES, FEATS)), dma((2, PIECES, FEATS)),
            dma((6,)),
        ],
        compiler_params=pltpu.CompilerParams(
            collective_id=0, has_side_effects=True, vmem_limit_bytes=60 * 2**20),
    )(batch_node_input, weight_in, second_layer_weight, send_rows[0], recv_rows[0], block_count[:, :, 0])


def solution(mesh):
    return jax.shard_map(
        per_device, mesh=mesh,
        in_specs=(P("node", "feat"), P("feat", None), P(), P("node", None, None), P("node", None, None), P("node", None, None)),
        out_specs=P("node", "feat"), check_vma=False)
```

```python
import functools

import jax
import jax.numpy as jnp
from jax import lax
from jax.experimental import pallas as pl
from jax.experimental.pallas import tpu as pltpu
from jax.sharding import PartitionSpec as P

MESH = pl.DeviceIdType.MESH
NZ, NY, NX, NC = 8, 4, 4, 2
NODES, FEATS = NZ * NY, NX * NC
PIECES = 2
BASE = 64
CAPS = (352, 304, 224, 128)
FEAT_STEPS = ((2, 0), (2, 1), (1, 0), (3, 0), (1, 1), (3, 1), (0, 1))
BF16, F32 = jnp.bfloat16, jnp.float32


def order(i):
    return lax.rem(4 + lax.rem(i, 2) * ((i + 1) // 2) - (1 - lax.rem(i, 2)) * (i // 2), NZ)


def kernel(packed, x_hbm, w1_hbm, w2_hbm, send_hbm, recv_hbm, count_hbm, out_ref, *refs):
    if packed:
        over_ref, *refs = refs
        (count_all, count_mat, spots, pack, unpack1, unpack2, unpack3, unpack4, parcel, hop1, hop2, hop3, hop4, handed,
         count_send, count_recv, hop_send, hop_recv, hand_send, hand_recv) = refs[27:]
        unpacks, hops = (unpack1, unpack2, unpack3, unpack4), (hop1, hop2, hop3, hop4)
    run(packed, x_hbm, w1_hbm, w2_hbm, send_hbm, recv_hbm, count_hbm, out_ref,
        *(refs[:27]), *((over_ref, count_all, count_mat, spots, pack, unpacks, parcel, hops, handed,
                         count_send, count_recv, hop_send, hop_recv, hand_send, hand_recv) if packed else (None,) * 15))


def run(
    packed, x_hbm, w1_hbm, w2_hbm, send_hbm, recv_hbm, count_hbm, out_ref,
    x_ref, send_ref, recv_ref, count_ref, w1_all, w2_all, out_slots, in_slots, send_cols, recv_live, pick, place,
    total, degree, mine, rows_in, rows_out, second,
    slot_send, slot_recv, w1_send, w1_recv, w1_send2, w1_recv2, row_send, row_recv, in_sem,
    over_ref, count_all, count_mat, spots, pack, unpacks, parcel, hops, handed,
    count_send, count_recv, hop_send, hop_recv, hand_send, hand_recv,
):
    rows, width = x_ref.shape
    slots = send_ref.shape[1]
    part = rows // FEATS
    node, feat = lax.axis_index("node"), lax.axis_index("feat")
    z, y = node // NY, lax.rem(node, NY)
    x, c = feat // NC, lax.rem(feat, NC)

    barrier = pltpu.get_barrier_semaphore()

    def greet_plane(i, _):
        zz = lax.rem(z + order(i), NZ)
        for j in range(NY):
            pl.semaphore_signal(barrier, inc=1, device_id=(zz * NY + j, feat), device_id_type=MESH)
        return 0

    lax.fori_loop(0, NZ - 1, greet_plane, 0)
    for j in range(1, NY):
        pl.semaphore_signal(
            barrier, inc=1, device_id=(z * NY + lax.rem(y + j, NY), feat), device_id_type=MESH)
    for d in range(1, FEATS):
        pl.semaphore_signal(
            barrier, inc=1, device_id=(node, lax.rem(feat + d, FEATS)), device_id_type=MESH)

    send_in = pltpu.make_async_copy(send_hbm, send_ref, in_sem.at[0])
    x_in = pltpu.make_async_copy(x_hbm, x_ref, in_sem.at[1])
    recv_in = pltpu.make_async_copy(recv_hbm, recv_ref, in_sem.at[2])
    count_in = pltpu.make_async_copy(count_hbm, count_ref, in_sem.at[3])
    w1_in = pltpu.make_async_copy(w1_hbm, w1_all.at[feat], in_sem.at[4])
    w2_in = pltpu.make_async_copy(w2_hbm, w2_all, in_sem.at[5])
    for copy in (send_in, x_in, recv_in, count_in, w1_in, w2_in):
        copy.start()

    def w1_copy(dx):
        return pltpu.make_async_remote_copy(
            w1_hbm, w1_all.at[feat], w1_send.at[dx], w1_recv.at[dx],
            device_id=(node, lax.rem(x + dx, NX) * NC + c), device_id_type=MESH)

    def w1_pass(dx):
        held = lax.rem(x + NX - dx, NX) * NC + c
        return pltpu.make_async_remote_copy(
            w1_hbm if dx == 0 else w1_all.at[held], w1_all.at[held], w1_send2.at[dx], w1_recv2.at[dx],
            device_id=(node, x * NC + 1 - c), device_id_type=MESH)

    base = BASE if packed else slots
    rest = slots - base

    def slot_copy(layer, other, count):
        return pltpu.make_async_remote_copy(
            out_slots.at[layer, other, pl.ds(0, count)], in_slots.at[layer, node, pl.ds(0, count)],
            slot_send.at[layer, other], slot_recv.at[layer, node],
            device_id=(other, feat), device_id_type=MESH)

    def slot_wait(layer, other, count):
        pltpu.make_async_remote_copy(
            out_slots.at[layer, other, pl.ds(0, count)], in_slots.at[layer, other, pl.ds(0, count)],
            slot_send.at[layer, other], slot_recv.at[layer, other],
            device_id=(other, feat), device_id_type=MESH).wait_recv()

    def build_pick(zz):
        cols = send_cols[...]
        lane = lax.broadcasted_iota(jnp.int32, cols.shape, 1)
        row_id = lax.broadcasted_iota(jnp.int32, (slots, rows), 1).astype(F32)
        for j in range(NY):
            col = jnp.sum(jnp.where(lane == zz * NY + j, cols, 0.0), axis=1, keepdims=True)
            pick[zz, j * slots:(j + 1) * slots, :] = jnp.where(row_id == col, 1.0, 0.0).astype(BF16)

    def select(layer, source, zz):
        if layer == 0:
            build_pick(zz)
        got = jnp.dot(pick[zz], source[...], preferred_element_type=F32).astype(BF16)
        out_slots[layer, pl.ds(zz * NY, NY)] = got.reshape(NY, slots, width)

    def send_plane(layer, zz, ys=range(NY)):
        for j in ys:
            slot_copy(layer, zz * NY + j, base).start()

    def near(i):
        return lax.rem(z + order(NZ - 2 - i), NZ)

    def send_rest(layer, source, first):
        def plane(i, _):
            select(layer, source, near(i))
            send_plane(layer, near(i))
            return 0

        lax.fori_loop(first, 4 if packed else NZ - 1, plane, 0)
        select(layer, source, z)
        for j in range(1, NY):
            slot_copy(layer, z * NY + lax.rem(y + j, NY), slots).start()
        in_slots[layer, node] = out_slots[layer, node]

    def build_place(zz, _):
        ids = recv_live[zz]
        row_id = lax.broadcasted_iota(jnp.int32, (rows, slots), 0)
        for j in range(NY):
            place[zz, :, j * slots:(j + 1) * slots] = jnp.where(
                row_id == ids[j:j + 1, :], 1.0, 0.0).astype(BF16)
        return 0

    def add_plane(layer, zz):
        held = in_slots[layer, pl.ds(zz * NY, NY)].reshape(NY * slots, width)
        if layer == 0:
            held = jnp.concatenate([held, jnp.ones_like(held)], axis=1)
            both = jnp.dot(place[zz], held, preferred_element_type=F32)
            total[...] += both[:, :width]
            degree[...] += both[:, width:]
        else:
            total[...] += jnp.dot(place[zz], held, preferred_element_type=F32)

    def add_near(layer):
        for j in range(1, NY):
            slot_wait(layer, z * NY + lax.rem(y + j, NY), slots)
        add_plane(layer, z)

    def add_far(layer, first, last):
        def plane(i, _):
            zz = lax.rem(z + NZ - order(NZ - 2 - i), NZ)
            for j in range(NY):
                slot_wait(layer, zz * NY + j, base)
            if packed:
                for j in range(1, NY):
                    hand_wait(layer, zz * NY + lax.rem(y + j, NY))
            add_plane(layer, zz)
            return 0

        lax.fori_loop(first, last, plane, 0)

    def count_copy(other):
        return pltpu.make_async_remote_copy(
            count_ref, count_all.at[node], count_send.at[other], count_recv.at[node],
            device_id=(other, feat), device_id_type=MESH)

    def count_wait(other):
        pltpu.make_async_remote_copy(
            count_ref, count_all.at[other], count_send.at[other], count_recv.at[other],
            device_id=(other, feat), device_id_type=MESH).wait_recv()

    def hop_copy(layer, way, h):
        source = parcel.at[layer, way] if h == 0 else hops[h - 1].at[layer, way, pl.ds(0, CAPS[h])]
        return pltpu.make_async_remote_copy(
            source, hops[h].at[layer, way], hop_send.at[layer, way, h], hop_recv.at[layer, way, h],
            device_id=(lax.rem(z + (1 if way == 0 else NZ - 1), NZ) * NY + y, feat), device_id_type=MESH)

    def origin(way, h):
        return lax.rem(z + (NZ - 1 - h if way == 0 else h + 1), NZ) * NY + y

    def hand_copy(layer, way, h, j):
        return pltpu.make_async_remote_copy(
            handed.at[layer, way, h, j], in_slots.at[layer, origin(way, h), pl.ds(base, rest)],
            hand_send.at[layer, way, h, j], hand_recv.at[layer, origin(way, h)],
            device_id=(z * NY + j, feat), device_id_type=MESH)

    def hand_wait(layer, other):
        pltpu.make_async_remote_copy(
            handed.at[layer, 0, 0, 0], in_slots.at[layer, other, pl.ds(base, rest)],
            hand_send.at[layer, 0, 0, 0], hand_recv.at[layer, other],
            device_id=(other, feat), device_id_type=MESH).wait_recv()

    def ends(way, h):
        return range(NY) if h < 3 else range(0, 2) if way == 0 else range(2, NY)

    def way_and_steps(there, here):
        step = (there // NY + NZ - here) & (NZ - 1)
        low = (there & (NY - 1)) < 2
        up = ((step >= 1) & (step <= 3)) | ((step == 4) & low)
        away = jnp.where(step <= 4, step, NZ - step)
        return jnp.where(step == 0, 2, jnp.where(up, 0, 1)), away

    def plan(source, ov, ov_t):
        here = source // NY
        square = (NODES, NODES)
        sub = lax.broadcasted_iota(jnp.int32, square, 0)
        lane = lax.broadcasted_iota(jnp.int32, square, 1)
        row = jnp.sum(jnp.where(sub == source, ov_t, 0.0), axis=0, keepdims=True)
        col = jnp.sum(jnp.where(lane == source, ov, 0.0), axis=1, keepdims=True)
        way, away = way_and_steps(sub, here)
        way_l, away_l = way_and_steps(lane, here)
        before = (way == way_l) & ((away_l > away) | ((away_l == away) & ((lane & (NY - 1)) < (sub & (NY - 1)))))
        offset = jnp.sum(jnp.where(before, row, 0.0), axis=1, keepdims=True)
        slot = lax.broadcasted_iota(jnp.int32, (NODES, slots), 1).astype(F32) - float(base)
        return jnp.where((slot >= 0.0) & (slot < col), offset + slot, -1.0)

    def prepare():
        lax.fori_loop(1, NODES, lambda k, _: (count_wait(lax.rem(node + k, NODES)), 0)[1], 0)
        count_mat[...] = jnp.zeros_like(count_mat)
        for p in range(NODES):
            count_mat[p:p + 1, :NODES] = count_all[p].astype(F32)
        ov_wide = jnp.maximum(count_mat[...] - float(base), 0.0)
        ov = ov_wide[:, :NODES]
        ov_t = ov_wide.T[:NODES, :]
        square = (NODES, NODES)
        sub = lax.broadcasted_iota(jnp.int32, square, 0)
        lane = lax.broadcasted_iota(jnp.int32, square, 1)
        way, away = way_and_steps(lane, sub // NY)
        worst = jnp.zeros((NODES, 1), F32)
        for w in range(2):
            for h in range(4):
                load = jnp.sum(jnp.where((way == w) & (away > h), ov_t, 0.0), axis=1, keepdims=True)
                worst = jnp.maximum(worst, load - float(CAPS[h]))
        over_ref[...] = jnp.zeros(over_ref.shape, F32) + jnp.max(worst, axis=0, keepdims=True)
        mine_spots = plan(node, ov, ov_t)
        for q in range(NZ):
            spots[q] = mine_spots[q * NY:(q + 1) * NY]
        for w in range(2):
            for h in range(4):
                ids = spots[lax.rem(z + (h + 1 if w == 0 else NZ - 1 - h), NZ)]
                row_id = lax.broadcasted_iota(jnp.int32, (CAPS[0], slots), 0).astype(F32)
                for j in ends(w, h):
                    pack[w, h, :, j * slots:(j + 1) * slots] = jnp.where(
                        row_id == ids[j:j + 1, :], 1.0, 0.0).astype(BF16)
        return ov, ov_t

    def prepare_unpack(ov, ov_t):
        for w in range(2):
            for h in range(4):
                columns = plan(origin(w, h), ov, ov_t).T
                lane = lax.broadcasted_iota(jnp.int32, columns.shape, 1)
                row_id = lax.broadcasted_iota(jnp.int32, (rest, CAPS[h]), 1).astype(F32)
                for j in ends(w, h):
                    col = jnp.sum(jnp.where(lane == z * NY + j, columns, 0.0), axis=1, keepdims=True)
                    unpacks[h][w, j * rest:(j + 1) * rest, :] = jnp.where(
                        row_id == col[base:, :], 1.0, 0.0).astype(BF16)

    def start_hops(layer):
        for w in range(2):
            got = jnp.zeros((CAPS[0], width), F32)
            for h in range(4):
                zz = lax.rem(z + (h + 1 if w == 0 else NZ - 1 - h), NZ)
                first, last = ends(w, h)[0], ends(w, h)[-1] + 1
                held = out_slots[layer, pl.ds(zz * NY + first, last - first)].reshape((last - first) * slots, width)
                got += jnp.dot(pack[w, h, :, first * slots:last * slots], held, preferred_element_type=F32)
            parcel[layer, w] = got.astype(BF16)
            hop_copy(layer, w, 0).start()

    def take_hop(layer, h):
        for w in range(2):
            hop_copy(layer, w, h).wait_recv()
            if h < 3:
                hop_copy(layer, w, h + 1).start()
        for w in range(2):
            first, last = ends(w, h)[0], ends(w, h)[-1] + 1
            got = jnp.dot(
                unpacks[h][w, first * rest:last * rest, :], hops[h][layer, w], preferred_element_type=F32).astype(BF16)
            for j in ends(w, h):
                handed[layer, w, h, j] = got[(j - first) * rest:(j - first + 1) * rest]

                @pl.when(y != j)
                def _():
                    hand_copy(layer, w, h, j).start()

                @pl.when(y == j)
                def _():
                    in_slots[layer, origin(w, h), base:] = got[(j - first) * rest:(j - first + 1) * rest]

    def sent_hops(layer):
        for w in range(2):
            for h in range(4):
                hop_copy(layer, w, h).wait_send()
                for j in ends(w, h):
                    @pl.when(y != j)
                    def _():
                        hand_copy(layer, w, h, j).wait_send()

    def select_last(layer, source):
        lax.fori_loop(4, NZ - 1, lambda i, _: (select(layer, source, near(i)), 0)[1], 0)

    def finish_packed(layer, middle=None):
        for zz in (near(4), near(5)):
            send_plane(layer, zz, (0, 1))
        if middle is not None:
            middle()
        add_near(layer)
        take_hop(layer, 0)
        for zz in (near(4), near(5)):
            send_plane(layer, zz, (2, 3))
        take_hop(layer, 1)
        send_plane(layer, near(6))
        add_far(layer, 0, 2)
        take_hop(layer, 2)
        add_far(layer, 2, 4)
        take_hop(layer, 3)
        if layer == 0:
            pass_w1()
        add_far(layer, 4, 7)

    def pass_w1():
        for dx in range(1, NX):
            w1_copy(dx).wait_recv()
            w1_pass(dx).start()

    early = 2
    count_in.wait()
    send_in.wait()
    send_cols[...] = send_ref[...].astype(F32).T
    x_in.wait()
    for i in range(early):
        select(0, x_ref, near(i))

    pl.semaphore_wait(barrier, NODES + FEATS - 2)

    if packed:
        def tell(i, _):
            for j in range(NY):
                count_copy(lax.rem(z + order(i), NZ) * NY + j).start()
            return 0

        lax.fori_loop(0, NZ - 1, tell, 0)
        for j in range(1, NY):
            count_copy(z * NY + lax.rem(y + j, NY)).start()
        count_all[node] = count_ref[...]
    for i in range(early):
        send_plane(0, near(i))
    for dx in range(1, NX):
        w1_copy(dx).start()
    w1_pass(0).start()

    send_rest(0, x_ref, early)

    def prepare_place():
        recv_in.wait()
        nodes = recv_ref.shape[0]
        across = (lax.broadcasted_iota(jnp.int32, (nodes, nodes), 0)
                  == lax.broadcasted_iota(jnp.int32, (nodes, nodes), 1))
        counts = jnp.sum(jnp.where(across, count_ref[...].astype(F32), 0.0), axis=1, keepdims=True)
        slot_id = lax.broadcasted_iota(jnp.int32, recv_ref.shape, 1).astype(F32)
        live = jnp.where(slot_id < counts, recv_ref[...], -1)
        for q in range(NZ):
            recv_live[q] = live[q * NY:(q + 1) * NY]
        lax.fori_loop(0, NZ, build_place, 0)
        degree[...] = jnp.ones_like(degree)
        total[...] = x_ref[...].astype(F32)

    if packed:
        select_last(0, x_ref)
        ov, ov_t = prepare()
        start_hops(0)

        def middle():
            prepare_unpack(ov, ov_t)
            prepare_place()

        finish_packed(0, middle)
    else:
        prepare_place()
        add_near(0)
        add_far(0, 0, 5)
        pass_w1()
        add_far(0, 5, 7)
    degree[...] = 1.0 / degree[...]
    mine[...] = (total[...] * degree[...]).astype(BF16)

    piece = part // PIECES

    def row_copy(step, h, d):
        dx, dc = FEAT_STEPS[d]
        other = lax.rem(x + dx, NX) * NC + lax.rem(c + dc, NC)
        if step == 0:
            source = mine.at[pl.ds(pl.multiple_of(other * part + h * piece, 16), piece)]
            target = rows_in.at[feat, pl.ds(h * piece, piece)]
        else:
            source = rows_out.at[other, pl.ds(h * piece, piece)]
            target = second.at[pl.ds(pl.multiple_of(feat * part + h * piece, 16), piece)]
        return pltpu.make_async_remote_copy(
            source, target, row_send.at[step, h, d], row_recv.at[step, h, d],
            device_id=(node, other), device_id_type=MESH)

    each = range(len(FEAT_STEPS))
    for h in range(PIECES):
        for d in each:
            row_copy(0, h, d).start()
    rows_in[feat] = mine[pl.ds(pl.multiple_of(feat * part, 16), part)]
    for dx in range(NX):
        w1_pass(dx).wait_recv()
    w1_in.wait()
    w2_in.wait()
    for h in range(PIECES):
        for d in each:
            row_copy(0, h, d).wait_recv()
        held = jnp.concatenate([rows_in[f, h * piece:(h + 1) * piece] for f in range(FEATS)], axis=1)
        hidden = jnp.dot(
            held, w1_all[...].reshape(FEATS * width, FEATS * width), preferred_element_type=F32)
        hidden = jnp.maximum(hidden, 0.0).astype(BF16)
        result = jnp.dot(hidden, w2_all[...], preferred_element_type=F32).astype(BF16)
        for f in range(FEATS):
            rows_out[f, h * piece:(h + 1) * piece] = result[:, f * width:(f + 1) * width]
        for d in each:
            row_copy(1, h, d).start()
    second[pl.ds(pl.multiple_of(feat * part, 16), part)] = rows_out[feat]
    for h in range(PIECES):
        for d in each:
            row_copy(1, h, d).wait_recv()

    send_rest(1, second, 0)
    total[...] = second[...].astype(F32)
    if packed:
        select_last(1, second)
        start_hops(1)
        finish_packed(1)
    else:
        add_near(1)
        add_far(1, 0, 7)
    out_ref[...] = (total[...] * degree[...]).astype(BF16)

    def sent(i, _):
        for j in range(NY):
            for layer in range(2):
                slot_copy(layer, near(i) * NY + j, base).wait_send()
            if packed:
                count_copy(near(i) * NY + j).wait_send()
        return 0

    lax.fori_loop(0, NZ - 1, sent, 0)
    for j in range(1, NY):
        other = z * NY + lax.rem(y + j, NY)
        for layer in range(2):
            slot_copy(layer, other, slots).wait_send()
        if packed:
            count_copy(other).wait_send()
    if packed:
        sent_hops(0)
        sent_hops(1)
    for dx in range(1, NX):
        w1_copy(dx).wait_send()
    for dx in range(NX):
        w1_pass(dx).wait_send()
    for h in range(PIECES):
        for d in each:
            row_copy(0, h, d).wait_send()
            row_copy(1, h, d).wait_send()


def layers(packed, batch_node_input, weight_in, second_layer_weight, send_rows, recv_rows, block_count):
    rows, width = batch_node_input.shape
    nodes, slots = send_rows.shape[1:]
    part = rows // FEATS
    hidden = weight_in.shape[1]
    vmem = pl.BlockSpec(memory_space=pltpu.VMEM)
    dma = pltpu.SemaphoreType.DMA
    out_shape = [jax.ShapeDtypeStruct((rows, width), BF16)]
    scratch = [
        pltpu.VMEM((rows, width), BF16),
        pltpu.VMEM((nodes, slots), jnp.int32),
        pltpu.VMEM((nodes, slots), jnp.int32),
        pltpu.VMEM((1, nodes), jnp.int32),
        pltpu.VMEM((FEATS, width, hidden), BF16),
        pltpu.VMEM((hidden, hidden), BF16),
        pltpu.VMEM((2, nodes, slots, width), BF16),
        pltpu.VMEM((2, nodes, slots, width), BF16),
        pltpu.VMEM((slots, nodes), F32),
        pltpu.VMEM((NZ, NY, slots), jnp.int32),
        pltpu.VMEM((NZ, NY * slots, rows), BF16),
        pltpu.VMEM((NZ, rows, NY * slots), BF16),
        pltpu.VMEM((rows, width), F32),
        pltpu.VMEM((rows, width), F32),
        pltpu.VMEM((rows, width), BF16),
        pltpu.VMEM((FEATS, part, width), BF16),
        pltpu.VMEM((FEATS, part, width), BF16),
        pltpu.VMEM((rows, width), BF16),
        dma((2, nodes)), dma((2, nodes)),
        dma((NX,)), dma((NX,)), dma((NX,)), dma((NX,)),
        dma((2, PIECES, FEATS)), dma((2, PIECES, FEATS)),
        dma((6,)),
    ]
    if packed:
        rest = slots - BASE
        out_shape.append(jax.ShapeDtypeStruct((8, 128), F32))
        scratch += [
            pltpu.VMEM((nodes, 1, nodes), jnp.int32),
            pltpu.VMEM((nodes, 128), F32),
            pltpu.VMEM((NZ, NY, slots), F32),
            pltpu.VMEM((2, 4, CAPS[0], NY * slots), BF16),
            *[pltpu.VMEM((2, NY * rest, cap), BF16) for cap in CAPS],
            pltpu.VMEM((2, 2, CAPS[0], width), BF16),
            *[pltpu.VMEM((2, 2, cap, width), BF16) for cap in CAPS],
            pltpu.VMEM((2, 2, 4, NY, rest, width), BF16),
            dma((nodes,)), dma((nodes,)),
            dma((2, 2, 4)), dma((2, 2, 4)),
            dma((2, 2, 4, NY)), dma((2, nodes)),
        ]
    return pl.pallas_call(
        functools.partial(kernel, packed),
        out_shape=out_shape,
        in_specs=[pl.BlockSpec(memory_space=pltpu.HBM)] * 6,
        out_specs=[vmem] * len(out_shape),
        scratch_shapes=scratch,
        compiler_params=pltpu.CompilerParams(
            collective_id=0 if packed else 1, has_side_effects=True, vmem_limit_bytes=60 * 2**20),
    )(batch_node_input, weight_in, second_layer_weight, send_rows[0], recv_rows[0], block_count[:, :, 0])


def per_device(*args):
    result, over = layers(True, *args)
    return lax.cond(over[0, 0] > 0.0, lambda: layers(False, *args)[0], lambda: result)


def solution(mesh):
    return jax.shard_map(
        per_device, mesh=mesh,
        in_specs=(P("node", "feat"), P("feat", None), P(), P("node", None, None), P("node", None, None), P("node", None, None)),
        out_specs=P("node", "feat"), check_vma=False)
```

```python
import functools

import jax
import jax.numpy as jnp
from jax import lax
from jax.experimental import pallas as pl
from jax.experimental.pallas import tpu as pltpu
from jax.sharding import PartitionSpec as P

MESH = pl.DeviceIdType.MESH
NZ, NY, NX, NC = 8, 4, 4, 2
NODES, FEATS = NZ * NY, NX * NC
PIECES = 2
FEAT_STEPS = ((2, 0), (2, 1), (1, 0), (3, 0), (1, 1), (3, 1), (0, 1))
BF16, F32 = jnp.bfloat16, jnp.float32


def order(i):
    return lax.rem(4 + lax.rem(i, 2) * ((i + 1) // 2) - (1 - lax.rem(i, 2)) * (i // 2), NZ)


def swap(v):
    half = v.shape[-1] // 2
    return jnp.concatenate([v[..., half:], v[..., :half]], axis=-1)


def low_lanes(v):
    return lax.broadcasted_iota(jnp.int32, v.shape, v.ndim - 1) < v.shape[-1] // 2


def join(a, b):
    return jnp.where(low_lanes(a), a, swap(b))


def join_high(a, b):
    return jnp.where(low_lanes(a), swap(a), b)


def pair(first, later, half):
    return join(first, later) if half == 0 else join_high(later, first)


def kernel(
    x_hbm, w1_hbm, w2_hbm, send_hbm, recv_hbm, count_hbm, out_ref,
    x_ref, send_ref, recv_ref, count_ref, w1_all, w2_all, out_slots, in_slots, send_cols, recv_live, pick, place,
    total, degree, mine, rows_in, rows_out, back, second, before,
    slot_send, slot_recv, w1_send, w1_recv, w1_send2, w1_recv2, row_send, row_recv, in_sem,
):
    rows, width = x_ref.shape
    slots = send_ref.shape[1]
    part = rows // FEATS
    near_slots = slots // 2
    node, feat = lax.axis_index("node"), lax.axis_index("feat")
    z, y = node // NY, lax.rem(node, NY)
    x, c = feat // NC, lax.rem(feat, NC)

    barrier = pltpu.get_barrier_semaphore()

    def greet_plane(i, _):
        zz = lax.rem(z + order(i), NZ)
        for j in range(NY):
            pl.semaphore_signal(barrier, inc=1, device_id=(zz * NY + j, feat), device_id_type=MESH)
        return 0

    lax.fori_loop(0, NZ - 1, greet_plane, 0)
    for j in range(1, NY):
        pl.semaphore_signal(
            barrier, inc=1, device_id=(z * NY + lax.rem(y + j, NY), feat), device_id_type=MESH)
    for d in range(1, FEATS):
        pl.semaphore_signal(
            barrier, inc=1, device_id=(node, lax.rem(feat + d, FEATS)), device_id_type=MESH)

    send_in = pltpu.make_async_copy(send_hbm, send_ref, in_sem.at[0])
    x_in = pltpu.make_async_copy(x_hbm, x_ref, in_sem.at[1])
    recv_in = pltpu.make_async_copy(recv_hbm, recv_ref, in_sem.at[2])
    count_in = pltpu.make_async_copy(count_hbm, count_ref, in_sem.at[3])
    w1_in = pltpu.make_async_copy(w1_hbm, w1_all.at[feat], in_sem.at[4])
    w2_in = pltpu.make_async_copy(w2_hbm, w2_all, in_sem.at[5])
    for copy in (send_in, x_in, recv_in, count_in, w1_in, w2_in):
        copy.start()

    def w1_copy(dx):
        return pltpu.make_async_remote_copy(
            w1_hbm, w1_all.at[feat], w1_send.at[dx], w1_recv.at[dx],
            device_id=(node, lax.rem(x + dx, NX) * NC + c), device_id_type=MESH)

    def w1_pass(dx):
        held = lax.rem(x + NX - dx, NX) * NC + c
        return pltpu.make_async_remote_copy(
            w1_hbm if dx == 0 else w1_all.at[held], w1_all.at[held], w1_send2.at[dx], w1_recv2.at[dx],
            device_id=(node, x * NC + 1 - c), device_id_type=MESH)

    def slot_copy(layer, half, other):
        k = 2 * layer + half
        return pltpu.make_async_remote_copy(
            out_slots.at[k, other], in_slots.at[k, node], slot_send.at[k, other], slot_recv.at[k, node],
            device_id=(other, feat), device_id_type=MESH)

    def slot_wait(layer, half, other):
        k = 2 * layer + half
        pltpu.make_async_remote_copy(
            out_slots.at[k, other], in_slots.at[k, other], slot_send.at[k, other], slot_recv.at[k, other],
            device_id=(other, feat), device_id_type=MESH).wait_recv()

    def build_pick(zz):
        cols = send_cols[...]
        lane = lax.broadcasted_iota(jnp.int32, cols.shape, 1)
        row_id = lax.broadcasted_iota(jnp.int32, (slots, rows), 1).astype(F32)
        for j in range(NY):
            col = jnp.sum(jnp.where(lane == zz * NY + j, cols, 0.0), axis=1, keepdims=True)
            hot = jnp.where(row_id == col, 1.0, 0.0).astype(BF16)
            for k in range(2):
                at = (k * NY + j) * near_slots
                pick[zz, at:at + near_slots, :] = hot[k * near_slots:(k + 1) * near_slots]

    def select(layer, halves, source, zz):
        if layer == 0:
            build_pick(zz)
        got = jnp.dot(pick[zz], source, preferred_element_type=F32).astype(BF16)
        for half in halves:
            packed = pair(got[:NY * near_slots], got[NY * near_slots:], half)
            out_slots[2 * layer + half, pl.ds(zz * NY, NY)] = packed.reshape(NY, near_slots, width)

    def send_plane(layer, half, zz):
        for j in (2, 1, 3, 0):
            slot_copy(layer, half, zz * NY + lax.rem(y + j, NY)).start()

    def near(i):
        return lax.rem(z + order(NZ - 2 - i), NZ)

    def send_own(layer, half):
        for j in (2, 1, 3):
            slot_copy(layer, half, z * NY + lax.rem(y + j, NY)).start()
        in_slots[2 * layer + half, node] = out_slots[2 * layer + half, node]

    def send_half(layer, half, halves, source, first):
        def plane(i, _):
            if halves:
                select(layer, halves, source[...], near(i))
            send_plane(layer, half, near(i))
            return 0

        lax.fori_loop(first, NZ - 1, plane, 0)
        if halves:
            select(layer, halves, source[...], z)
        send_own(layer, half)

    def build_place(zz, _):
        ids = recv_live[zz]
        row_id = lax.broadcasted_iota(jnp.int32, (rows, slots), 0)
        for j in range(NY):
            place[zz, :, j * slots:(j + 1) * slots] = jnp.where(
                row_id == ids[:, j * slots:(j + 1) * slots], 1.0, 0.0).astype(BF16)
        degree[...] += jnp.dot(
            place[zz], jnp.ones((NY * slots, width), BF16), preferred_element_type=F32)
        return 0

    def add_plane(layer, half, zz):
        held = in_slots[2 * layer + half, pl.ds(zz * NY, NY)].reshape(NY * near_slots, width)
        held = jnp.concatenate([held, swap(held)], axis=0)
        total[half] += jnp.dot(place[zz], held, preferred_element_type=F32)

    def add_own(layer, half):
        for j in range(1, NY):
            slot_wait(layer, half, z * NY + lax.rem(y + j, NY))
        add_plane(layer, half, z)

    def add_far(layer, half, first, last):
        def plane(i, _):
            zz = lax.rem(z + NZ - order(NZ - 2 - i), NZ)
            for j in range(NY):
                slot_wait(layer, half, zz * NY + j)
            add_plane(layer, half, zz)
            return 0

        lax.fori_loop(first, last, plane, 0)

    def pass_w1():
        for dx in range(1, NX):
            w1_copy(dx).wait_recv()
            w1_pass(dx).start()

    early = 2
    send_in.wait()
    send_cols[...] = send_ref[...].astype(F32).T
    x_in.wait()
    for i in range(early):
        select(0, (0, 1), x_ref[...], near(i))

    pl.semaphore_wait(barrier, NODES + FEATS - 2)

    for i in range(early):
        send_plane(0, 0, near(i))
    for dx in range(1, NX):
        w1_copy(dx).start()
    w1_pass(0).start()

    send_half(0, 0, (0, 1), x_ref, early)
    send_half(0, 1, (), x_ref, 0)

    recv_in.wait()
    count_in.wait()
    nodes = recv_ref.shape[0]
    across = (lax.broadcasted_iota(jnp.int32, (nodes, nodes), 0)
              == lax.broadcasted_iota(jnp.int32, (nodes, nodes), 1))
    counts = jnp.sum(jnp.where(across, count_ref[...].astype(F32), 0.0), axis=1, keepdims=True)
    slot_id = lax.broadcasted_iota(jnp.int32, recv_ref.shape, 1).astype(F32)
    live = jnp.where(slot_id < counts, recv_ref[...], -1)
    for q in range(NZ):
        blocks = [live[q * NY + j:q * NY + j + 1] for j in range(NY)]
        recv_live[q] = jnp.concatenate(
            [b[:, :near_slots] for b in blocks] + [b[:, near_slots:] for b in blocks], axis=1)
    degree[...] = jnp.ones_like(degree)
    lax.fori_loop(0, NZ, build_place, 0)
    degree[...] = 1.0 / degree[...]

    low = part // 2
    piece = low // PIECES

    def row_copy(step, half, h, d):
        dx, dc = FEAT_STEPS[d]
        other = lax.rem(x + dx, NX) * NC + lax.rem(c + dc, NC)
        source = (mine if step == 0 else rows_out).at[half, other, pl.ds(h * piece, piece)]
        target = (rows_in if step == 0 else back).at[half, feat, pl.ds(h * piece, piece)]
        k = 2 * step + half
        return pltpu.make_async_remote_copy(
            source, target, row_send.at[k, h, d], row_recv.at[k, h, d],
            device_id=(node, other), device_id_type=MESH)

    each = range(len(FEAT_STEPS))

    def send_rows(half):
        scaled = (total[half] * degree[...]).astype(BF16)
        for f in range(FEATS):
            mine[half, f] = pair(scaled[f * part:f * part + low], scaled[f * part + low:(f + 1) * part], half)
        for h in range(PIECES):
            for d in each:
                row_copy(0, half, h, d).start()
        rows_in[half, feat] = mine[half, feat]

    def multiply(half, h):
        got = [rows_in[half, f, h * piece:(h + 1) * piece] for f in range(FEATS)]
        pairs = [(got[f], got[f + 1]) for f in range(0, FEATS, 2)]
        lows = jnp.concatenate([join(*p) for p in pairs], axis=1)
        highs = jnp.concatenate([join_high(*p) for p in pairs], axis=1)
        held = jnp.concatenate([lows, highs] if half == 0 else [highs, lows], axis=0)
        span = slice(0, width // 2) if half == 0 else slice(width // 2, width)
        weight = w1_all[:, span, :].reshape(FEATS * width // 2, FEATS * width)
        return jnp.dot(held, weight, preferred_element_type=F32)

    for half in range(2):
        total[half] = x_ref[...].astype(F32)
    add_own(0, 0)
    add_far(0, 0, 0, 5)
    pass_w1()
    add_far(0, 0, 5, 7)
    send_rows(0)
    add_own(0, 1)
    add_far(0, 1, 0, 4)
    for dx in range(NX):
        w1_pass(dx).wait_recv()
    w1_in.wait()
    w2_in.wait()
    for h in range(PIECES):
        for d in each:
            row_copy(0, 0, h, d).wait_recv()
        before[h] = multiply(0, h)
    add_far(0, 1, 4, 7)
    send_rows(1)
    for h in range(PIECES):
        for d in each:
            row_copy(0, 1, h, d).wait_recv()
        hidden = jnp.maximum(before[h] + multiply(1, h), 0.0).astype(BF16)
        result = jnp.dot(hidden, w2_all[...], preferred_element_type=F32).astype(BF16)
        for half in range(2):
            for f in range(FEATS):
                block = result[:, f * width:(f + 1) * width]
                rows_out[half, f, h * piece:(h + 1) * piece] = pair(block[:piece], block[piece:], half)
        for d in each:
            row_copy(1, 0, h, d).start()
    for h in range(PIECES):
        for d in each:
            row_copy(1, 1, h, d).start()

    for half in range(2):
        back[half, feat] = rows_out[half, feat]
        for h in range(PIECES):
            for d in each:
                row_copy(1, half, h, d).wait_recv()
        for f in range(FEATS):
            got = back[half, f]
            second[half, f * part:f * part + low] = got
            second[half, f * part + low:(f + 1) * part] = swap(got)
        send_half(1, half, (half,), second.at[half], 0)
    for half in range(2):
        total[half] = second[half].astype(F32)
        add_own(1, half)
        add_far(1, half, 0, 7)
    out_ref[...] = (jnp.where(low_lanes(total[0]), total[0], total[1]) * degree[...]).astype(BF16)

    def sent(k, _):
        other = lax.rem(node + k, NODES)
        for layer in range(2):
            for half in range(2):
                slot_copy(layer, half, other).wait_send()
        return 0

    lax.fori_loop(1, NODES, sent, 0)
    for dx in range(1, NX):
        w1_copy(dx).wait_send()
    for dx in range(NX):
        w1_pass(dx).wait_send()
    for h in range(PIECES):
        for d in each:
            for step in range(2):
                for half in range(2):
                    row_copy(step, half, h, d).wait_send()


def per_device(batch_node_input, weight_in, second_layer_weight, send_rows, recv_rows, block_count):
    rows, width = batch_node_input.shape
    nodes, slots = send_rows.shape[1:]
    part = rows // FEATS
    hidden = weight_in.shape[1]
    vmem = pl.BlockSpec(memory_space=pltpu.VMEM)
    dma = pltpu.SemaphoreType.DMA
    return pl.pallas_call(
        kernel,
        out_shape=jax.ShapeDtypeStruct((rows, width), BF16),
        in_specs=[pl.BlockSpec(memory_space=pltpu.HBM)] * 6,
        out_specs=vmem,
        scratch_shapes=[
            pltpu.VMEM((rows, width), BF16),
            pltpu.VMEM((nodes, slots), jnp.int32),
            pltpu.VMEM((nodes, slots), jnp.int32),
            pltpu.VMEM((1, nodes), jnp.int32),
            pltpu.VMEM((FEATS, width, hidden), BF16),
            pltpu.VMEM((hidden, hidden), BF16),
            pltpu.VMEM((4, nodes, slots // 2, width), BF16),
            pltpu.VMEM((4, nodes, slots // 2, width), BF16),
            pltpu.VMEM((slots, nodes), F32),
            pltpu.VMEM((NZ, 1, NY * slots), jnp.int32),
            pltpu.VMEM((NZ, NY * slots, rows), BF16),
            pltpu.VMEM((NZ, rows, NY * slots), BF16),
            pltpu.VMEM((2, rows, width), F32),
            pltpu.VMEM((rows, width), F32),
            pltpu.VMEM((2, FEATS, part // 2, width), BF16),
            pltpu.VMEM((2, FEATS, part // 2, width), BF16),
            pltpu.VMEM((2, FEATS, part // 2, width), BF16),
            pltpu.VMEM((2, FEATS, part // 2, width), BF16),
            pltpu.VMEM((2, rows, width), BF16),
            pltpu.VMEM((PIECES, part // PIECES, hidden), F32),
            dma((4, nodes)), dma((4, nodes)),
            dma((NX,)), dma((NX,)), dma((NX,)), dma((NX,)),
            dma((4, PIECES, FEATS)), dma((4, PIECES, FEATS)),
            dma((6,)),
        ],
        compiler_params=pltpu.CompilerParams(
            collective_id=0, has_side_effects=True, vmem_limit_bytes=60 * 2**20),
    )(batch_node_input, weight_in, second_layer_weight, send_rows[0], recv_rows[0], block_count[:, :, 0])


def solution(mesh):
    return jax.shard_map(
        per_device, mesh=mesh,
        in_specs=(P("node", "feat"), P("feat", None), P(), P("node", None, None), P("node", None, None), P("node", None, None)),
        out_specs=P("node", "feat"), check_vma=False)
```

```python
import functools

import jax
import jax.numpy as jnp
from jax import lax
from jax.experimental import pallas as pl
from jax.experimental.pallas import tpu as pltpu
from jax.sharding import PartitionSpec as P

MESH = pl.DeviceIdType.MESH
NZ, NY, NX, NC = 8, 4, 4, 2
NODES, FEATS = NZ * NY, NX * NC
PIECES = 1
FEAT_STEPS = ((2, 1), (1, 1), (3, 1), (2, 0), (1, 0), (3, 0), (0, 1))
BF16, F32 = jnp.bfloat16, jnp.float32


def order(i):
    return lax.rem(4 + lax.rem(i, 2) * ((i + 1) // 2) - (1 - lax.rem(i, 2)) * (i // 2), NZ)


def kernel(
    x_hbm, w1_hbm, w2_hbm, send_hbm, recv_hbm, count_hbm, out_ref,
    x_ref, send_ref, recv_ref, count_ref, w1_all, w2_all, out_slots, in_slots, send_cols, recv_live, pick, place,
    total, degree, mine, rows_in, rows_out, second,
    slot_send, slot_recv, w1_send, w1_recv, w1_send2, w1_recv2, row_send, row_recv, in_sem,
):
    rows, width = x_ref.shape
    slots = send_ref.shape[1]
    part = rows // FEATS
    node, feat = lax.axis_index("node"), lax.axis_index("feat")
    z, y = node // NY, lax.rem(node, NY)
    x, c = feat // NC, lax.rem(feat, NC)

    barrier = pltpu.get_barrier_semaphore()

    def greet_plane(i, _):
        zz = lax.rem(z + order(i), NZ)
        for j in range(NY):
            pl.semaphore_signal(barrier, inc=1, device_id=(zz * NY + j, feat), device_id_type=MESH)
        return 0

    lax.fori_loop(0, NZ - 1, greet_plane, 0)
    for j in range(1, NY):
        pl.semaphore_signal(
            barrier, inc=1, device_id=(z * NY + lax.rem(y + j, NY), feat), device_id_type=MESH)
    for d in range(1, FEATS):
        pl.semaphore_signal(
            barrier, inc=1, device_id=(node, lax.rem(feat + d, FEATS)), device_id_type=MESH)

    send_in = pltpu.make_async_copy(send_hbm, send_ref, in_sem.at[0])
    x_in = pltpu.make_async_copy(x_hbm, x_ref, in_sem.at[1])
    recv_in = pltpu.make_async_copy(recv_hbm, recv_ref, in_sem.at[2])
    count_in = pltpu.make_async_copy(count_hbm, count_ref, in_sem.at[3])
    w1_in = pltpu.make_async_copy(w1_hbm, w1_all.at[feat], in_sem.at[4])
    w2_in = pltpu.make_async_copy(w2_hbm, w2_all, in_sem.at[5])
    for copy in (send_in, x_in, recv_in, count_in, w1_in, w2_in):
        copy.start()

    def w1_copy(dx):
        return pltpu.make_async_remote_copy(
            w1_hbm, w1_all.at[feat], w1_send.at[dx], w1_recv.at[dx],
            device_id=(node, lax.rem(x + dx, NX) * NC + c), device_id_type=MESH)

    def w1_pass(dx):
        held = lax.rem(x + NX - dx, NX) * NC + c
        return pltpu.make_async_remote_copy(
            w1_hbm if dx == 0 else w1_all.at[held], w1_all.at[held], w1_send2.at[dx], w1_recv2.at[dx],
            device_id=(node, x * NC + 1 - c), device_id_type=MESH)

    def slot_copy(layer, other):
        return pltpu.make_async_remote_copy(
            out_slots.at[layer, other], in_slots.at[layer, node],
            slot_send.at[layer, other], slot_recv.at[layer, node],
            device_id=(other, feat), device_id_type=MESH)

    def slot_wait(layer, other):
        pltpu.make_async_remote_copy(
            out_slots.at[layer, other], in_slots.at[layer, other],
            slot_send.at[layer, other], slot_recv.at[layer, other],
            device_id=(other, feat), device_id_type=MESH).wait_recv()

    def build_pick(zz):
        cols = send_cols[...]
        lane = lax.broadcasted_iota(jnp.int32, cols.shape, 1)
        row_id = lax.broadcasted_iota(jnp.int32, (slots, rows), 1).astype(F32)
        for j in range(NY):
            col = jnp.sum(jnp.where(lane == zz * NY + j, cols, 0.0), axis=1, keepdims=True)
            pick[zz, j * slots:(j + 1) * slots, :] = jnp.where(row_id == col, 1.0, 0.0).astype(BF16)

    def select(layer, source, zz):
        if layer == 0:
            build_pick(zz)
        got = jnp.dot(pick[zz], source[...], preferred_element_type=F32).astype(BF16)
        out_slots[layer, pl.ds(zz * NY, NY)] = got.reshape(NY, slots, width)

    def send_plane(layer, zz):
        for j in (2, 1, 3, 0):
            slot_copy(layer, zz * NY + lax.rem(y + j, NY)).start()

    def near(i):
        return lax.rem(z + order(NZ - 2 - i), NZ)

    def send_rest(layer, source, first):
        def plane(i, _):
            select(layer, source, near(i))
            send_plane(layer, near(i))
            return 0

        lax.fori_loop(first, NZ - 1, plane, 0)
        select(layer, source, z)
        for j in range(1, NY):
            slot_copy(layer, z * NY + lax.rem(y + j, NY)).start()
        in_slots[layer, node] = out_slots[layer, node]

    def build_place(zz, _):
        ids = recv_live[zz]
        row_id = lax.broadcasted_iota(jnp.int32, (rows, slots), 0)
        for j in range(NY):
            place[zz, :, j * slots:(j + 1) * slots] = jnp.where(
                row_id == ids[j:j + 1, :], 1.0, 0.0).astype(BF16)
        degree[...] += jnp.dot(
            place[zz], jnp.ones((NY * slots, width), BF16), preferred_element_type=F32)
        return 0

    def add_plane(layer, zz):
        held = in_slots[layer, pl.ds(zz * NY, NY)].reshape(NY * slots, width)
        total[...] += jnp.dot(place[zz], held, preferred_element_type=F32)

    def add_all(layer, middle=None):
        for j in range(1, NY):
            slot_wait(layer, z * NY + lax.rem(y + j, NY))
        add_plane(layer, z)

        def plane(i, _):
            zz = lax.rem(z + NZ - order(NZ - 2 - i), NZ)
            for j in range(NY):
                slot_wait(layer, zz * NY + j)
            add_plane(layer, zz)
            return 0

        if middle is None:
            lax.fori_loop(0, NZ - 1, plane, 0)
        else:
            lax.fori_loop(0, NZ - 3, plane, 0)
            middle()
            lax.fori_loop(NZ - 3, NZ - 1, plane, 0)

    def pass_w1():
        for dx in range(1, NX):
            w1_copy(dx).wait_recv()
            w1_pass(dx).start()

    early = 2
    send_in.wait()
    send_cols[...] = send_ref[...].astype(F32).T
    x_in.wait()
    for i in range(early):
        select(0, x_ref, near(i))

    pl.semaphore_wait(barrier, NODES + FEATS - 2)

    for i in range(early):
        send_plane(0, near(i))
    for dx in range(1, NX):
        w1_copy(dx).start()
    w1_pass(0).start()

    send_rest(0, x_ref, early)

    recv_in.wait()
    count_in.wait()
    nodes = recv_ref.shape[0]
    across = (lax.broadcasted_iota(jnp.int32, (nodes, nodes), 0)
              == lax.broadcasted_iota(jnp.int32, (nodes, nodes), 1))
    counts = jnp.sum(jnp.where(across, count_ref[...].astype(F32), 0.0), axis=1, keepdims=True)
    slot_id = lax.broadcasted_iota(jnp.int32, recv_ref.shape, 1).astype(F32)
    live = jnp.where(slot_id < counts, recv_ref[...], -1)
    for q in range(NZ):
        recv_live[q] = live[q * NY:(q + 1) * NY]
    degree[...] = jnp.ones_like(degree)
    lax.fori_loop(0, NZ, build_place, 0)
    degree[...] = 1.0 / degree[...]

    total[...] = x_ref[...].astype(F32)
    add_all(0, pass_w1)
    mine[...] = (total[...] * degree[...]).astype(BF16)

    piece = part // PIECES

    def row_copy(step, h, d):
        dx, dc = FEAT_STEPS[d]
        other = lax.rem(x + dx, NX) * NC + lax.rem(c + dc, NC)
        if step == 0:
            source = mine.at[pl.ds(pl.multiple_of(other * part + h * piece, 16), piece)]
            target = rows_in.at[feat, pl.ds(h * piece, piece)]
        else:
            source = rows_out.at[other, pl.ds(h * piece, piece)]
            target = second.at[pl.ds(pl.multiple_of(feat * part + h * piece, 16), piece)]
        return pltpu.make_async_remote_copy(
            source, target, row_send.at[step, h, d], row_recv.at[step, h, d],
            device_id=(node, other), device_id_type=MESH)

    each = range(len(FEAT_STEPS))
    for h in range(PIECES):
        for d in each:
            row_copy(0, h, d).start()
    rows_in[feat] = mine[pl.ds(pl.multiple_of(feat * part, 16), part)]
    for dx in range(NX):
        w1_pass(dx).wait_recv()
    w1_in.wait()
    w2_in.wait()
    for h in range(PIECES):
        for d in each:
            row_copy(0, h, d).wait_recv()
        held = jnp.concatenate([rows_in[f, h * piece:(h + 1) * piece] for f in range(FEATS)], axis=1)
        hidden = jnp.dot(
            held, w1_all[...].reshape(FEATS * width, FEATS * width), preferred_element_type=F32)
        hidden = jnp.maximum(hidden, 0.0).astype(BF16)
        result = jnp.dot(hidden, w2_all[...], preferred_element_type=F32).astype(BF16)
        for f in range(FEATS):
            rows_out[f, h * piece:(h + 1) * piece] = result[:, f * width:(f + 1) * width]
        for d in each:
            row_copy(1, h, d).start()
    second[pl.ds(pl.multiple_of(feat * part, 16), part)] = rows_out[feat]
    for h in range(PIECES):
        for d in each:
            row_copy(1, h, d).wait_recv()

    send_rest(1, second, 0)
    total[...] = second[...].astype(F32)
    add_all(1)
    out_ref[...] = (total[...] * degree[...]).astype(BF16)

    def sent(k, _):
        other = lax.rem(node + k, NODES)
        slot_copy(0, other).wait_send()
        slot_copy(1, other).wait_send()
        return 0

    lax.fori_loop(1, NODES, sent, 0)
    for dx in range(1, NX):
        w1_copy(dx).wait_send()
    for dx in range(NX):
        w1_pass(dx).wait_send()
    for h in range(PIECES):
        for d in each:
            row_copy(0, h, d).wait_send()
            row_copy(1, h, d).wait_send()


def per_device(batch_node_input, weight_in, second_layer_weight, send_rows, recv_rows, block_count):
    rows, width = batch_node_input.shape
    nodes, slots = send_rows.shape[1:]
    part = rows // FEATS
    hidden = weight_in.shape[1]
    vmem = pl.BlockSpec(memory_space=pltpu.VMEM)
    dma = pltpu.SemaphoreType.DMA
    return pl.pallas_call(
        kernel,
        out_shape=jax.ShapeDtypeStruct((rows, width), BF16),
        in_specs=[pl.BlockSpec(memory_space=pltpu.HBM)] * 6,
        out_specs=vmem,
        scratch_shapes=[
            pltpu.VMEM((rows, width), BF16),
            pltpu.VMEM((nodes, slots), jnp.int32),
            pltpu.VMEM((nodes, slots), jnp.int32),
            pltpu.VMEM((1, nodes), jnp.int32),
            pltpu.VMEM((FEATS, width, hidden), BF16),
            pltpu.VMEM((hidden, hidden), BF16),
            pltpu.VMEM((2, nodes, slots, width), BF16),
            pltpu.VMEM((2, nodes, slots, width), BF16),
            pltpu.VMEM((slots, nodes), F32),
            pltpu.VMEM((NZ, NY, slots), jnp.int32),
            pltpu.VMEM((NZ, NY * slots, rows), BF16),
            pltpu.VMEM((NZ, rows, NY * slots), BF16),
            pltpu.VMEM((rows, width), F32),
            pltpu.VMEM((rows, width), F32),
            pltpu.VMEM((rows, width), BF16),
            pltpu.VMEM((FEATS, part, width), BF16),
            pltpu.VMEM((FEATS, part, width), BF16),
            pltpu.VMEM((rows, width), BF16),
            dma((2, nodes)), dma((2, nodes)),
            dma((NX,)), dma((NX,)), dma((NX,)), dma((NX,)),
            dma((2, PIECES, FEATS)), dma((2, PIECES, FEATS)),
            dma((6,)),
        ],
        compiler_params=pltpu.CompilerParams(
            collective_id=0, has_side_effects=True, vmem_limit_bytes=60 * 2**20),
    )(batch_node_input, weight_in, second_layer_weight, send_rows[0], recv_rows[0], block_count[:, :, 0])


def solution(mesh):
    return jax.shard_map(
        per_device, mesh=mesh,
        in_specs=(P("node", "feat"), P("feat", None), P(), P("node", None, None), P("node", None, None), P("node", None, None)),
        out_specs=P("node", "feat"), check_vma=False)
```

```python
import functools

import jax
import jax.numpy as jnp
from jax import lax
from jax.experimental import pallas as pl
from jax.experimental.pallas import tpu as pltpu
from jax.sharding import PartitionSpec as P

MESH = pl.DeviceIdType.MESH
NZ, NY, NX, NC = 8, 4, 4, 2
NODES, FEATS = NZ * NY, NX * NC
PIECES = 1
FEAT_STEPS = ((2, 1), (1, 1), (3, 1), (2, 0), (1, 0), (3, 0), (0, 1))
BF16, F32 = jnp.bfloat16, jnp.float32


def order(i):
    return lax.rem(4 + lax.rem(i, 2) * ((i + 1) // 2) - (1 - lax.rem(i, 2)) * (i // 2), NZ)


def kernel(
    x_hbm, w1_hbm, w2_hbm, send_hbm, recv_hbm, count_hbm, out_ref,
    x_ref, send_ref, recv_ref, count_ref, w1_all, w2_all, out_slots, in_slots, send_cols, recv_live, pick, place,
    total, degree, mine, rows_in, rows_out, second,
    slot_send, slot_recv, w1_send, w1_recv, w1_send2, w1_recv2, row_send, row_recv, in_sem,
):
    rows, width = x_ref.shape
    slots = send_ref.shape[1]
    part = rows // FEATS
    node, feat = lax.axis_index("node"), lax.axis_index("feat")
    z, y = node // NY, lax.rem(node, NY)
    x, c = feat // NC, lax.rem(feat, NC)

    barrier = pltpu.get_barrier_semaphore()

    def greet_plane(i, _):
        zz = lax.rem(z + order(i), NZ)
        for j in range(NY):
            pl.semaphore_signal(barrier, inc=1, device_id=(zz * NY + j, feat), device_id_type=MESH)
        return 0

    lax.fori_loop(0, NZ - 1, greet_plane, 0)
    for j in range(1, NY):
        pl.semaphore_signal(
            barrier, inc=1, device_id=(z * NY + lax.rem(y + j, NY), feat), device_id_type=MESH)
    for d in range(1, FEATS):
        pl.semaphore_signal(
            barrier, inc=1, device_id=(node, lax.rem(feat + d, FEATS)), device_id_type=MESH)

    send_in = pltpu.make_async_copy(send_hbm, send_ref, in_sem.at[0])
    x_in = pltpu.make_async_copy(x_hbm, x_ref, in_sem.at[1])
    recv_in = pltpu.make_async_copy(recv_hbm, recv_ref, in_sem.at[2])
    count_in = pltpu.make_async_copy(count_hbm, count_ref, in_sem.at[3])
    w1_in = pltpu.make_async_copy(w1_hbm, w1_all.at[feat], in_sem.at[4])
    w2_in = pltpu.make_async_copy(w2_hbm, w2_all, in_sem.at[5])
    for copy in (send_in, x_in, recv_in, count_in, w1_in, w2_in):
        copy.start()

    def w1_copy(dx):
        return pltpu.make_async_remote_copy(
            w1_hbm, w1_all.at[feat], w1_send.at[dx], w1_recv.at[dx],
            device_id=(node, lax.rem(x + dx, NX) * NC + c), device_id_type=MESH)

    def w1_pass(dx):
        held = lax.rem(x + NX - dx, NX) * NC + c
        return pltpu.make_async_remote_copy(
            w1_hbm if dx == 0 else w1_all.at[held], w1_all.at[held], w1_send2.at[dx], w1_recv2.at[dx],
            device_id=(node, x * NC + 1 - c), device_id_type=MESH)

    def slot_copy(layer, other):
        return pltpu.make_async_remote_copy(
            out_slots.at[layer, other], in_slots.at[layer, node],
            slot_send.at[layer, other], slot_recv.at[layer, node],
            device_id=(other, feat), device_id_type=MESH)

    def slot_wait(layer, other):
        pltpu.make_async_remote_copy(
            out_slots.at[layer, other], in_slots.at[layer, other],
            slot_send.at[layer, other], slot_recv.at[layer, other],
            device_id=(other, feat), device_id_type=MESH).wait_recv()

    def build_pick(zz):
        cols = send_cols[...]
        lane = lax.broadcasted_iota(jnp.int32, cols.shape, 1)
        row_id = lax.broadcasted_iota(jnp.int32, (slots, rows), 1).astype(F32)
        for j in range(NY):
            col = jnp.sum(jnp.where(lane == zz * NY + j, cols, 0.0), axis=1, keepdims=True)
            pick[zz, j * slots:(j + 1) * slots, :] = jnp.where(row_id == col, 1.0, 0.0).astype(BF16)

    def select(layer, source, zz):
        if layer == 0:
            build_pick(zz)
        got = jnp.dot(pick[zz], source[...], preferred_element_type=F32).astype(BF16)
        out_slots[layer, pl.ds(zz * NY, NY)] = got.reshape(NY, slots, width)

    def send_plane(layer, zz):
        for j in (2, 1, 3, 0):
            slot_copy(layer, zz * NY + lax.rem(y + j, NY)).start()

    def near(i):
        return lax.rem(z + order(NZ - 2 - lax.rem(i + 2, NZ - 1)), NZ)

    def send_rest(layer, source, first):
        def plane(i, _):
            select(layer, source, near(i))
            send_plane(layer, near(i))
            return 0

        lax.fori_loop(first, NZ - 1, plane, 0)
        select(layer, source, z)
        for j in range(1, NY):
            slot_copy(layer, z * NY + lax.rem(y + j, NY)).start()
        in_slots[layer, node] = out_slots[layer, node]

    def build_place(zz, _):
        ids = recv_live[zz]
        row_id = lax.broadcasted_iota(jnp.int32, (rows, slots), 0)
        for j in range(NY):
            place[zz, :, j * slots:(j + 1) * slots] = jnp.where(
                row_id == ids[j:j + 1, :], 1.0, 0.0).astype(BF16)
        degree[...] += jnp.dot(
            place[zz], jnp.ones((NY * slots, width), BF16), preferred_element_type=F32)
        return 0

    def add_plane(layer, zz):
        held = in_slots[layer, pl.ds(zz * NY, NY)].reshape(NY * slots, width)
        total[...] += jnp.dot(place[zz], held, preferred_element_type=F32)

    def add_all(layer, middle=None):
        for j in range(1, NY):
            slot_wait(layer, z * NY + lax.rem(y + j, NY))
        add_plane(layer, z)

        def plane(i, _):
            zz = lax.rem(z + NZ - order(NZ - 2 - lax.rem(i + 2, NZ - 1)), NZ)
            for j in range(NY):
                slot_wait(layer, zz * NY + j)
            add_plane(layer, zz)
            return 0

        if middle is None:
            lax.fori_loop(0, NZ - 1, plane, 0)
        else:
            lax.fori_loop(0, NZ - 3, plane, 0)
            middle()
            lax.fori_loop(NZ - 3, NZ - 1, plane, 0)

    def pass_w1():
        for dx in range(1, NX):
            w1_copy(dx).wait_recv()
            w1_pass(dx).start()

    early = 2
    send_in.wait()
    send_cols[...] = send_ref[...].astype(F32).T
    x_in.wait()
    for i in range(early):
        select(0, x_ref, near(i))

    pl.semaphore_wait(barrier, NODES + FEATS - 2)

    for i in range(early):
        send_plane(0, near(i))
    for dx in range(1, NX):
        w1_copy(dx).start()
    w1_pass(0).start()

    send_rest(0, x_ref, early)

    recv_in.wait()
    count_in.wait()
    nodes = recv_ref.shape[0]
    across = (lax.broadcasted_iota(jnp.int32, (nodes, nodes), 0)
              == lax.broadcasted_iota(jnp.int32, (nodes, nodes), 1))
    counts = jnp.sum(jnp.where(across, count_ref[...].astype(F32), 0.0), axis=1, keepdims=True)
    slot_id = lax.broadcasted_iota(jnp.int32, recv_ref.shape, 1).astype(F32)
    live = jnp.where(slot_id < counts, recv_ref[...], -1)
    for q in range(NZ):
        recv_live[q] = live[q * NY:(q + 1) * NY]
    degree[...] = jnp.ones_like(degree)
    lax.fori_loop(0, NZ, build_place, 0)
    degree[...] = 1.0 / degree[...]

    total[...] = x_ref[...].astype(F32)
    add_all(0, pass_w1)
    mine[...] = (total[...] * degree[...]).astype(BF16)

    piece = part // PIECES

    def row_copy(step, h, d):
        dx, dc = FEAT_STEPS[d]
        other = lax.rem(x + dx, NX) * NC + lax.rem(c + dc, NC)
        if step == 0:
            source = mine.at[pl.ds(pl.multiple_of(other * part + h * piece, 16), piece)]
            target = rows_in.at[feat, pl.ds(h * piece, piece)]
        else:
            source = rows_out.at[other, pl.ds(h * piece, piece)]
            target = second.at[pl.ds(pl.multiple_of(feat * part + h * piece, 16), piece)]
        return pltpu.make_async_remote_copy(
            source, target, row_send.at[step, h, d], row_recv.at[step, h, d],
            device_id=(node, other), device_id_type=MESH)

    each = range(len(FEAT_STEPS))
    for h in range(PIECES):
        for d in each:
            row_copy(0, h, d).start()
    rows_in[feat] = mine[pl.ds(pl.multiple_of(feat * part, 16), part)]
    for dx in range(NX):
        w1_pass(dx).wait_recv()
    w1_in.wait()
    w2_in.wait()
    for h in range(PIECES):
        for d in each:
            row_copy(0, h, d).wait_recv()
        held = jnp.concatenate([rows_in[f, h * piece:(h + 1) * piece] for f in range(FEATS)], axis=1)
        hidden = jnp.dot(
            held, w1_all[...].reshape(FEATS * width, FEATS * width), preferred_element_type=F32)
        hidden = jnp.maximum(hidden, 0.0).astype(BF16)
        result = jnp.dot(hidden, w2_all[...], preferred_element_type=F32).astype(BF16)
        for f in range(FEATS):
            rows_out[f, h * piece:(h + 1) * piece] = result[:, f * width:(f + 1) * width]
        for d in each:
            row_copy(1, h, d).start()
    second[pl.ds(pl.multiple_of(feat * part, 16), part)] = rows_out[feat]
    for h in range(PIECES):
        for d in each:
            row_copy(1, h, d).wait_recv()

    send_rest(1, second, 0)
    total[...] = second[...].astype(F32)
    add_all(1)
    out_ref[...] = (total[...] * degree[...]).astype(BF16)

    def sent(k, _):
        other = lax.rem(node + k, NODES)
        slot_copy(0, other).wait_send()
        slot_copy(1, other).wait_send()
        return 0

    lax.fori_loop(1, NODES, sent, 0)
    for dx in range(1, NX):
        w1_copy(dx).wait_send()
    for dx in range(NX):
        w1_pass(dx).wait_send()
    for h in range(PIECES):
        for d in each:
            row_copy(0, h, d).wait_send()
            row_copy(1, h, d).wait_send()


def per_device(batch_node_input, weight_in, second_layer_weight, send_rows, recv_rows, block_count):
    rows, width = batch_node_input.shape
    nodes, slots = send_rows.shape[1:]
    part = rows // FEATS
    hidden = weight_in.shape[1]
    vmem = pl.BlockSpec(memory_space=pltpu.VMEM)
    dma = pltpu.SemaphoreType.DMA
    return pl.pallas_call(
        kernel,
        out_shape=jax.ShapeDtypeStruct((rows, width), BF16),
        in_specs=[pl.BlockSpec(memory_space=pltpu.HBM)] * 6,
        out_specs=vmem,
        scratch_shapes=[
            pltpu.VMEM((rows, width), BF16),
            pltpu.VMEM((nodes, slots), jnp.int32),
            pltpu.VMEM((nodes, slots), jnp.int32),
            pltpu.VMEM((1, nodes), jnp.int32),
            pltpu.VMEM((FEATS, width, hidden), BF16),
            pltpu.VMEM((hidden, hidden), BF16),
            pltpu.VMEM((2, nodes, slots, width), BF16),
            pltpu.VMEM((2, nodes, slots, width), BF16),
            pltpu.VMEM((slots, nodes), F32),
            pltpu.VMEM((NZ, NY, slots), jnp.int32),
            pltpu.VMEM((NZ, NY * slots, rows), BF16),
            pltpu.VMEM((NZ, rows, NY * slots), BF16),
            pltpu.VMEM((rows, width), F32),
            pltpu.VMEM((rows, width), F32),
            pltpu.VMEM((rows, width), BF16),
            pltpu.VMEM((FEATS, part, width), BF16),
            pltpu.VMEM((FEATS, part, width), BF16),
            pltpu.VMEM((rows, width), BF16),
            dma((2, nodes)), dma((2, nodes)),
            dma((NX,)), dma((NX,)), dma((NX,)), dma((NX,)),
            dma((2, PIECES, FEATS)), dma((2, PIECES, FEATS)),
            dma((6,)),
        ],
        compiler_params=pltpu.CompilerParams(
            collective_id=0, has_side_effects=True, vmem_limit_bytes=60 * 2**20),
    )(batch_node_input, weight_in, second_layer_weight, send_rows[0], recv_rows[0], block_count[:, :, 0])


def solution(mesh):
    return jax.shard_map(
        per_device, mesh=mesh,
        in_specs=(P("node", "feat"), P("feat", None), P(), P("node", None, None), P("node", None, None), P("node", None, None)),
        out_specs=P("node", "feat"), check_vma=False)
```

```python
import functools

import jax
import jax.numpy as jnp
from jax import lax
from jax.experimental import pallas as pl
from jax.experimental.pallas import tpu as pltpu
from jax.sharding import PartitionSpec as P

MESH = pl.DeviceIdType.MESH
NZ, NY, NX, NC = 8, 4, 4, 2
NODES, FEATS = NZ * NY, NX * NC
PIECES = 1
FEAT_STEPS = ((2, 1), (1, 1), (3, 1), (2, 0), (1, 0), (3, 0), (0, 1))
BF16, F32 = jnp.bfloat16, jnp.float32


def order(i):
    return lax.rem(4 + lax.rem(i, 2) * ((i + 1) // 2) - (1 - lax.rem(i, 2)) * (i // 2), NZ)


def kernel(
    x_hbm, w1_hbm, w2_hbm, send_hbm, recv_hbm, count_hbm, out_ref,
    x_ref, send_ref, recv_ref, count_ref, w1_all, w2_all, out_slots, in_slots, send_cols, recv_live, pick, place,
    total, degree, mine, rows_in, rows_out, second,
    slot_send, slot_recv, w1_send, w1_recv, w1_send2, w1_recv2, row_send, row_recv, in_sem,
):
    rows, width = x_ref.shape
    slots = send_ref.shape[1]
    part = rows // FEATS
    node, feat = lax.axis_index("node"), lax.axis_index("feat")
    z, y = node // NY, lax.rem(node, NY)
    x, c = feat // NC, lax.rem(feat, NC)

    barrier = pltpu.get_barrier_semaphore()

    def greet_plane(i, _):
        zz = lax.rem(z + order(i), NZ)
        for j in range(NY):
            pl.semaphore_signal(barrier, inc=1, device_id=(zz * NY + j, feat), device_id_type=MESH)
        return 0

    lax.fori_loop(0, NZ - 1, greet_plane, 0)
    for j in range(1, NY):
        pl.semaphore_signal(
            barrier, inc=1, device_id=(z * NY + lax.rem(y + j, NY), feat), device_id_type=MESH)
    for d in range(1, FEATS):
        pl.semaphore_signal(
            barrier, inc=1, device_id=(node, lax.rem(feat + d, FEATS)), device_id_type=MESH)

    send_in = pltpu.make_async_copy(send_hbm, send_ref, in_sem.at[0])
    x_in = pltpu.make_async_copy(x_hbm, x_ref, in_sem.at[1])
    recv_in = pltpu.make_async_copy(recv_hbm, recv_ref, in_sem.at[2])
    count_in = pltpu.make_async_copy(count_hbm, count_ref, in_sem.at[3])
    w1_in = pltpu.make_async_copy(w1_hbm, w1_all.at[feat], in_sem.at[4])
    w2_in = pltpu.make_async_copy(w2_hbm, w2_all, in_sem.at[5])
    for copy in (send_in, x_in, recv_in, count_in, w1_in, w2_in):
        copy.start()

    def w1_copy(dx):
        return pltpu.make_async_remote_copy(
            w1_hbm, w1_all.at[feat], w1_send.at[dx], w1_recv.at[dx],
            device_id=(node, lax.rem(x + dx, NX) * NC + c), device_id_type=MESH)

    def w1_pass(dx):
        held = lax.rem(x + NX - dx, NX) * NC + c
        return pltpu.make_async_remote_copy(
            w1_hbm if dx == 0 else w1_all.at[held], w1_all.at[held], w1_send2.at[dx], w1_recv2.at[dx],
            device_id=(node, x * NC + 1 - c), device_id_type=MESH)

    def slot_copy(layer, other):
        return pltpu.make_async_remote_copy(
            out_slots.at[layer, other], in_slots.at[layer, node],
            slot_send.at[layer, other], slot_recv.at[layer, node],
            device_id=(other, feat), device_id_type=MESH)

    def slot_wait(layer, other):
        pltpu.make_async_remote_copy(
            out_slots.at[layer, other], in_slots.at[layer, other],
            slot_send.at[layer, other], slot_recv.at[layer, other],
            device_id=(other, feat), device_id_type=MESH).wait_recv()

    def build_pick(zz):
        cols = send_cols[...]
        lane = lax.broadcasted_iota(jnp.int32, cols.shape, 1)
        row_id = lax.broadcasted_iota(jnp.int32, (slots, rows), 1).astype(F32)
        for j in range(NY):
            col = jnp.sum(jnp.where(lane == zz * NY + j, cols, 0.0), axis=1, keepdims=True)
            pick[zz, j * slots:(j + 1) * slots, :] = jnp.where(row_id == col, 1.0, 0.0).astype(BF16)

    def select(layer, source, zz):
        if layer == 0:
            build_pick(zz)
        got = jnp.dot(pick[zz], source[...], preferred_element_type=F32).astype(BF16)
        out_slots[layer, pl.ds(zz * NY, NY)] = got.reshape(NY, slots, width)

    def send_plane(layer, zz):
        for j in (2, 1, 3, 0):
            slot_copy(layer, zz * NY + lax.rem(y + j, NY)).start()

    def near(i):
        return lax.rem(z + order(NZ - 2 - lax.rem(i + 2, NZ - 1)), NZ)

    def send_rest(layer, source, first):
        def plane(i, _):
            select(layer, source, near(i))
            send_plane(layer, near(i))
            return 0

        lax.fori_loop(first, NZ - 3, plane, 0)
        select(layer, source, z)
        for j in range(1, NY):
            slot_copy(layer, z * NY + lax.rem(y + j, NY)).start()
        in_slots[layer, node] = out_slots[layer, node]
        lax.fori_loop(NZ - 3, NZ - 1, plane, 0)

    def build_place(zz, _):
        ids = recv_live[zz]
        row_id = lax.broadcasted_iota(jnp.int32, (rows, slots), 0)
        for j in range(NY):
            place[zz, :, j * slots:(j + 1) * slots] = jnp.where(
                row_id == ids[j:j + 1, :], 1.0, 0.0).astype(BF16)
        degree[...] += jnp.dot(
            place[zz], jnp.ones((NY * slots, width), BF16), preferred_element_type=F32)
        return 0

    def add_plane(layer, zz):
        held = in_slots[layer, pl.ds(zz * NY, NY)].reshape(NY * slots, width)
        total[...] += jnp.dot(place[zz], held, preferred_element_type=F32)

    def add_all(layer, middle=None):
        def plane(i, _):
            zz = lax.rem(z + NZ - order(NZ - 2 - lax.rem(i + 2, NZ - 1)), NZ)
            for j in range(NY):
                slot_wait(layer, zz * NY + j)
            add_plane(layer, zz)
            return 0

        lax.fori_loop(0, NZ - 3, plane, 0)
        if middle is not None:
            middle()
        for j in range(1, NY):
            slot_wait(layer, z * NY + lax.rem(y + j, NY))
        add_plane(layer, z)
        lax.fori_loop(NZ - 3, NZ - 1, plane, 0)

    def pass_w1():
        for dx in range(1, NX):
            w1_copy(dx).wait_recv()
            w1_pass(dx).start()

    early = 2
    send_in.wait()
    send_cols[...] = send_ref[...].astype(F32).T
    x_in.wait()
    for i in range(early):
        select(0, x_ref, near(i))

    pl.semaphore_wait(barrier, NODES + FEATS - 2)

    for i in range(early):
        send_plane(0, near(i))
    for dx in range(1, NX):
        w1_copy(dx).start()
    w1_pass(0).start()

    send_rest(0, x_ref, early)

    recv_in.wait()
    count_in.wait()
    nodes = recv_ref.shape[0]
    across = (lax.broadcasted_iota(jnp.int32, (nodes, nodes), 0)
              == lax.broadcasted_iota(jnp.int32, (nodes, nodes), 1))
    counts = jnp.sum(jnp.where(across, count_ref[...].astype(F32), 0.0), axis=1, keepdims=True)
    slot_id = lax.broadcasted_iota(jnp.int32, recv_ref.shape, 1).astype(F32)
    live = jnp.where(slot_id < counts, recv_ref[...], -1)
    for q in range(NZ):
        recv_live[q] = live[q * NY:(q + 1) * NY]
    degree[...] = jnp.ones_like(degree)
    lax.fori_loop(0, NZ, build_place, 0)
    degree[...] = 1.0 / degree[...]

    total[...] = x_ref[...].astype(F32)
    add_all(0, pass_w1)
    mine[...] = (total[...] * degree[...]).astype(BF16)

    piece = part // PIECES

    def row_copy(step, h, d):
        dx, dc = FEAT_STEPS[d]
        other = lax.rem(x + dx, NX) * NC + lax.rem(c + dc, NC)
        if step == 0:
            source = mine.at[pl.ds(pl.multiple_of(other * part + h * piece, 16), piece)]
            target = rows_in.at[feat, pl.ds(h * piece, piece)]
        else:
            source = rows_out.at[other, pl.ds(h * piece, piece)]
            target = second.at[pl.ds(pl.multiple_of(feat * part + h * piece, 16), piece)]
        return pltpu.make_async_remote_copy(
            source, target, row_send.at[step, h, d], row_recv.at[step, h, d],
            device_id=(node, other), device_id_type=MESH)

    each = range(len(FEAT_STEPS))
    for h in range(PIECES):
        for d in each:
            row_copy(0, h, d).start()
    rows_in[feat] = mine[pl.ds(pl.multiple_of(feat * part, 16), part)]
    for dx in range(NX):
        w1_pass(dx).wait_recv()
    w1_in.wait()
    w2_in.wait()
    for h in range(PIECES):
        for d in each:
            row_copy(0, h, d).wait_recv()
        held = jnp.concatenate([rows_in[f, h * piece:(h + 1) * piece] for f in range(FEATS)], axis=1)
        hidden = jnp.dot(
            held, w1_all[...].reshape(FEATS * width, FEATS * width), preferred_element_type=F32)
        hidden = jnp.maximum(hidden, 0.0).astype(BF16)
        result = jnp.dot(hidden, w2_all[...], preferred_element_type=F32).astype(BF16)
        for f in range(FEATS):
            rows_out[f, h * piece:(h + 1) * piece] = result[:, f * width:(f + 1) * width]
        for d in each:
            row_copy(1, h, d).start()
    second[pl.ds(pl.multiple_of(feat * part, 16), part)] = rows_out[feat]
    for h in range(PIECES):
        for d in each:
            row_copy(1, h, d).wait_recv()

    send_rest(1, second, 0)
    total[...] = second[...].astype(F32)
    add_all(1)
    out_ref[...] = (total[...] * degree[...]).astype(BF16)

    def sent(k, _):
        other = lax.rem(node + k, NODES)
        slot_copy(0, other).wait_send()
        slot_copy(1, other).wait_send()
        return 0

    lax.fori_loop(1, NODES, sent, 0)
    for dx in range(1, NX):
        w1_copy(dx).wait_send()
    for dx in range(NX):
        w1_pass(dx).wait_send()
    for h in range(PIECES):
        for d in each:
            row_copy(0, h, d).wait_send()
            row_copy(1, h, d).wait_send()


def per_device(batch_node_input, weight_in, second_layer_weight, send_rows, recv_rows, block_count):
    rows, width = batch_node_input.shape
    nodes, slots = send_rows.shape[1:]
    part = rows // FEATS
    hidden = weight_in.shape[1]
    vmem = pl.BlockSpec(memory_space=pltpu.VMEM)
    dma = pltpu.SemaphoreType.DMA
    return pl.pallas_call(
        kernel,
        out_shape=jax.ShapeDtypeStruct((rows, width), BF16),
        in_specs=[pl.BlockSpec(memory_space=pltpu.HBM)] * 6,
        out_specs=vmem,
        scratch_shapes=[
            pltpu.VMEM((rows, width), BF16),
            pltpu.VMEM((nodes, slots), jnp.int32),
            pltpu.VMEM((nodes, slots), jnp.int32),
            pltpu.VMEM((1, nodes), jnp.int32),
            pltpu.VMEM((FEATS, width, hidden), BF16),
            pltpu.VMEM((hidden, hidden), BF16),
            pltpu.VMEM((2, nodes, slots, width), BF16),
            pltpu.VMEM((2, nodes, slots, width), BF16),
            pltpu.VMEM((slots, nodes), F32),
            pltpu.VMEM((NZ, NY, slots), jnp.int32),
            pltpu.VMEM((NZ, NY * slots, rows), BF16),
            pltpu.VMEM((NZ, rows, NY * slots), BF16),
            pltpu.VMEM((rows, width), F32),
            pltpu.VMEM((rows, width), F32),
            pltpu.VMEM((rows, width), BF16),
            pltpu.VMEM((FEATS, part, width), BF16),
            pltpu.VMEM((FEATS, part, width), BF16),
            pltpu.VMEM((rows, width), BF16),
            dma((2, nodes)), dma((2, nodes)),
            dma((NX,)), dma((NX,)), dma((NX,)), dma((NX,)),
            dma((2, PIECES, FEATS)), dma((2, PIECES, FEATS)),
            dma((6,)),
        ],
        compiler_params=pltpu.CompilerParams(
            collective_id=0, has_side_effects=True, vmem_limit_bytes=60 * 2**20),
    )(batch_node_input, weight_in, second_layer_weight, send_rows[0], recv_rows[0], block_count[:, :, 0])


def solution(mesh):
    return jax.shard_map(
        per_device, mesh=mesh,
        in_specs=(P("node", "feat"), P("feat", None), P(), P("node", None, None), P("node", None, None), P("node", None, None)),
        out_specs=P("node", "feat"), check_vma=False)
```
